32 devices in a mesh: span: 2 (over x), seq: 16 (over z, y, core).
Axes of the slice: x: 2, y: 2, z: 4, core: 2. Of those that a mesh axis runs over, the one named last changes fastest.
Arguments:
- queries: bfloat16 [1536, 3072], P(('span', 'seq')), may hold values from -6 to 6
- keyvals: bfloat16 [1536, 1024], P(('span', 'seq')), may hold values from -6 to 6
- clip_index: int32 [2], replicated, may hold values from 0 to 7, as said below
- noise_step: int32 [2], replicated, may hold values from 0 to 63
- valid_count: int32 [2], replicated, may hold values from 384 to 768
- gate_table: float32 [64, 3072], replicated, may hold values from 0.5 to 2
Outputs:
- attended: bfloat16 [1536, 3072], P(('span', 'seq'))
The draws below stay inside these ranges and needn't reach their ends.
Inputs may be any that keep to these rules, and one draw needn't show every extreme that they name: `clip_index`: each group has a different clip index; some group's clip index is 7.
All inputs are finite; a program needn't handle non-finite values.
Results may differ from the reference program's by a relative error of at most 0.0044.
Values may be sent and summed in bfloat16 or wider, within the bound.
No kernel may reach another device: no remote copies, remote signals or barrier semaphores. Data moves between devices by JAX's collectives and lax.ppermute only.
A program may use at most 128 MiB of HBM per device.

```python
import math
import jax
import jax.numpy as jnp
from jax import lax

QUERY_HEADS = 24
KEY_VALUE_HEADS = 4
HEAD_WIDTH = 128
STEPS = 64
TOK_DEV = 48
SPAN_TOK = 768
ROWS = 1536
QW = 3072
KW = 512
N_SPAN = 2
N_SEQ = 16


def draw_clip_index(key, part):
    fresh = jax.random.fold_in(key, 31)
    key_pick, key_order = jax.random.split(fresh, 2)
    largest = 4 * N_SPAN - 1
    others = jax.random.permutation(key_pick, largest)[:N_SPAN - 1].astype(jnp.int32)
    values = jnp.concatenate([others, jnp.full((1,), largest, jnp.int32)])
    order = jax.random.permutation(key_order, N_SPAN)
    return values[order].astype(jnp.int32)


def draw_queries(key, part):
    fresh = jax.random.fold_in(key, 11)
    values = jnp.clip(jax.random.normal(fresh, (ROWS, QW), jnp.float32) * 1.7, -6.0, 6.0)
    return values.astype(jnp.bfloat16)


def draw_keyvals(key, part):
    fresh_key = jax.random.fold_in(key, 21)
    fresh_value = jax.random.fold_in(key, 22)
    key_portion = jnp.clip(jax.random.normal(fresh_key, (ROWS, KW), jnp.float32) * 1.7, -6.0, 6.0)
    value_part = jnp.clip(jax.random.normal(fresh_value, (ROWS, KW), jnp.float32), -6.0, 6.0)
    return jnp.concatenate([key_portion, value_part], axis=1).astype(jnp.bfloat16)


def setup_inputs(seed: int = 0) -> dict:
    streams_of = jax.random.split(jax.random.key(seed), 7)
    return {
        "queries": draw_queries(jax.random.fold_in(streams_of[6], 71), 0),
        "keyvals": draw_keyvals(jax.random.fold_in(streams_of[6], 71), 0),
        "clip_index": draw_clip_index(jax.random.fold_in(streams_of[6], 71), 0),
        "noise_step": jax.random.randint(streams_of[3], (N_SPAN,), 0, STEPS).astype(jnp.int32),
        "valid_count": jax.random.randint(streams_of[4], (N_SPAN,), SPAN_TOK // 2, SPAN_TOK + 1).astype(jnp.int32),
        "gate_table": jnp.clip(jnp.exp(jax.random.uniform(streams_of[5], (STEPS, QW), jnp.float32, math.log(0.5), math.log(2.0))), 0.5, 2.0),
    }


def reference(queries, keyvals, clip_index, noise_step, valid_count, gate_table):
    span_token_count = TOK_DEV * N_SEQ
    query_per_key_ratio = QUERY_HEADS // KEY_VALUE_HEADS
    key_row_width = KEY_VALUE_HEADS * HEAD_WIDTH
    inv_root = 1.0 / math.sqrt(HEAD_WIDTH)
    negative = -1e+30
    visible = clip_index[None, :] <= clip_index[:, None]
    positions = jnp.arange(span_token_count, dtype=jnp.int32)
    key_live = positions[None, :] < valid_count[:, None]
    key_row_block = keyvals[:, :key_row_width].reshape(N_SPAN * span_token_count, KEY_VALUE_HEADS, HEAD_WIDTH)
    value_row_block = keyvals[:, key_row_width:].reshape(N_SPAN * span_token_count, KEY_VALUE_HEADS, HEAD_WIDTH)
    query_row_block = queries.reshape(N_SPAN, span_token_count, KEY_VALUE_HEADS, query_per_key_ratio, HEAD_WIDTH)

    def attend_group(index_pair):
        group_id, kv_head = index_pair
        usable = (visible[group_id][:, None] & key_live).reshape(N_SPAN * span_token_count)
        query_part = query_row_block[group_id][:, kv_head].astype(jnp.float32)
        key_portion = key_row_block[:, kv_head].astype(jnp.float32)
        value_part = value_row_block[:, kv_head].astype(jnp.float32)
        scores = jnp.einsum('lrd,jd->rlj', query_part, key_portion) * inv_root
        scores = jnp.where(usable, scores, negative)
        row_max = scores.max(-1, keepdims=True)
        weights = jnp.where(usable, jnp.exp(scores - row_max), 0.0)
        weight_sum = weights.sum(-1)
        rounded = lax.optimization_barrier(weights.astype(jnp.bfloat16)).astype(jnp.float32)
        numerator = jnp.einsum('rlj,jd->rld', rounded, value_part)
        return numerator / weight_sum[..., None]
    group_numbers = jnp.repeat(jnp.arange(N_SPAN, dtype=jnp.int32), KEY_VALUE_HEADS)
    head_numbers = jnp.tile(jnp.arange(KEY_VALUE_HEADS, dtype=jnp.int32), N_SPAN)
    attended = lax.map(attend_group, (group_numbers, head_numbers))
    attended = attended.reshape(N_SPAN, KEY_VALUE_HEADS, query_per_key_ratio, span_token_count, HEAD_WIDTH).transpose(0, 3, 1, 2, 4)
    attended = attended.reshape(N_SPAN, span_token_count, QUERY_HEADS * HEAD_WIDTH)
    gate_rows = gate_table[noise_step]
    live_rows = key_live.astype(jnp.float32)[..., None]
    result = attended * gate_rows[:, None, :] * live_rows
    return result.reshape(N_SPAN * span_token_count, QUERY_HEADS * HEAD_WIDTH).astype(jnp.bfloat16)
```

```python
import functools
import math

import jax
import jax.numpy as jnp
import numpy as np
from jax import lax
from jax.experimental import pallas as pl
from jax.experimental.pallas import tpu as pltpu
from jax.sharding import PartitionSpec as P

QUERY_HEADS = 24
KEY_VALUE_HEADS = 4
HEAD_WIDTH = 128
RATIO = QUERY_HEADS // KEY_VALUE_HEADS
KEY_WIDTH = KEY_VALUE_HEADS * HEAD_WIDTH
NEGATIVE = -1e30
LOG2E = math.log2(math.e)
TILE = 384
MOST_PARTNERS = 3


def attend_kernel(n_kv, carried, last, place_ref, q_ref, *refs):
    kv_refs, bias_refs, refs = refs[:n_kv], refs[n_kv : 2 * n_kv], refs[2 * n_kv :]
    state_in = None
    if carried:
        state_in, refs = refs[:3], refs[3:]
    if last:
        gate_ref, out_ref = refs
    else:
        state_out = refs
    tokens = q_ref.shape[0]
    rows = RATIO * tokens
    scale = LOG2E / math.sqrt(HEAD_WIDTH)
    if last:
        positions = place_ref[0] + lax.broadcasted_iota(jnp.int32, (tokens, 1), 0)
        live = (positions < place_ref[1]).astype(jnp.float32)
    for head in range(KEY_VALUE_HEADS):
        first = head * RATIO
        query = jnp.concatenate(
            [
                q_ref[:, (first + r) * HEAD_WIDTH : (first + r + 1) * HEAD_WIDTH]
                for r in range(RATIO)
            ],
            axis=0,
        )

        def step(kv_ref, bias_ref, start, size, state):
            key = kv_ref[pl.ds(start, size), head * HEAD_WIDTH : (head + 1) * HEAD_WIDTH]
            value = kv_ref[
                pl.ds(start, size),
                KEY_WIDTH + head * HEAD_WIDTH : KEY_WIDTH + (head + 1) * HEAD_WIDTH,
            ]
            scores = lax.dot_general(
                query, key, (((1,), (1,)), ((), ())), preferred_element_type=jnp.float32
            )
            scores = scores * scale + bias_ref[:, pl.ds(start, size)]
            top = jnp.max(scores, axis=1, keepdims=True)
            if state is not None:
                top = jnp.maximum(top, state[0])
            weights = jnp.exp2(scores - top)
            total = jnp.sum(weights, axis=1, keepdims=True)
            numerator = jnp.dot(
                weights.astype(jnp.bfloat16), value, preferred_element_type=jnp.float32
            )
            if state is not None:
                factor = jnp.exp2(state[0] - top)
                total = total + state[1] * factor
                numerator = numerator + state[2] * factor
            return top, total, numerator

        span = pl.ds(head * rows, rows)
        state = tuple(ref[span, :] for ref in state_in) if carried else None
        for kv_ref, bias_ref in zip(kv_refs, bias_refs):
            state = step(kv_ref, bias_ref, 0, kv_ref.shape[0], state)
        if not last:
            for ref, part in zip(state_out, state):
                ref[span, :] = part
            continue
        result = state[2] * (1.0 / state[1])
        for r in range(RATIO):
            columns = slice((first + r) * HEAD_WIDTH, (first + r + 1) * HEAD_WIDTH)
            part = result[r * tokens : (r + 1) * tokens]
            out_ref[:, columns] = (part * gate_ref[:, columns] * live).astype(out_ref.dtype)


def attend(place, queries, keyvals, biases, state=None, gate=None):
    tokens = queries.shape[0]
    rows = QUERY_HEADS * tokens
    keys = sum(kv.shape[0] for kv in keyvals)
    last = gate is not None
    operands = [place, queries, *keyvals, *biases, *(state or ())] + ([gate] if last else [])
    whole = pl.BlockSpec(memory_space=pltpu.VMEM)
    if last:
        out_shape = jax.ShapeDtypeStruct(queries.shape, jnp.bfloat16)
    else:
        out_shape = (
            jax.ShapeDtypeStruct((rows, 1), jnp.float32),
            jax.ShapeDtypeStruct((rows, 1), jnp.float32),
            jax.ShapeDtypeStruct((rows, HEAD_WIDTH), jnp.float32),
        )
    return pl.pallas_call(
        functools.partial(attend_kernel, len(keyvals), state is not None, last),
        out_shape=out_shape,
        in_specs=[pl.BlockSpec(memory_space=pltpu.SMEM)] + [whole] * (len(operands) - 1),
        out_specs=whole if last else (whole,) * 3,
        compiler_params=pltpu.CompilerParams(vmem_limit_bytes=40 * 1024 * 1024),
        cost_estimate=pl.CostEstimate(
            flops=4 * rows * keys * HEAD_WIDTH,
            bytes_accessed=keys * 2 * KEY_WIDTH * 2,
            transcendentals=rows * keys,
        ),
    )(*operands)


def streamed_kernel(place_ref, q_ref, kv_ref, bias_ref, gate_ref, out_ref, top_ref, total_ref, numerator_ref):
    tokens = q_ref.shape[0]
    rows = RATIO * tokens
    scale = LOG2E / math.sqrt(HEAD_WIDTH)

    @pl.when(pl.program_id(0) == 0)
    def _():
        top_ref[...] = jnp.full_like(top_ref, NEGATIVE)
        total_ref[...] = jnp.zeros_like(total_ref)
        numerator_ref[...] = jnp.zeros_like(numerator_ref)

    for head in range(KEY_VALUE_HEADS):
        first = head * RATIO
        span = slice(head * rows, (head + 1) * rows)
        columns = [slice((first + r) * HEAD_WIDTH, (first + r + 1) * HEAD_WIDTH) for r in range(RATIO)]
        query = jnp.concatenate([q_ref[:, c] for c in columns], axis=0)
        key = kv_ref[:, head * HEAD_WIDTH : (head + 1) * HEAD_WIDTH]
        value = kv_ref[:, KEY_WIDTH + head * HEAD_WIDTH : KEY_WIDTH + (head + 1) * HEAD_WIDTH]
        scores = lax.dot_general(
            query, key, (((1,), (1,)), ((), ())), preferred_element_type=jnp.float32
        )
        scores = scores * scale + bias_ref[...]
        top = jnp.maximum(top_ref[span, :], jnp.max(scores, axis=1, keepdims=True))
        weights = jnp.exp2(scores - top)
        factor = jnp.exp2(top_ref[span, :] - top)
        top_ref[span, :] = top
        total_ref[span, :] = total_ref[span, :] * factor + jnp.sum(weights, axis=1, keepdims=True)
        numerator_ref[span, :] = numerator_ref[span, :] * factor + jnp.dot(
            weights.astype(jnp.bfloat16), value, preferred_element_type=jnp.float32
        )

    @pl.when(pl.program_id(0) == pl.num_programs(0) - 1)
    def _():
        positions = place_ref[0] + lax.broadcasted_iota(jnp.int32, (tokens, 1), 0)
        live = (positions < place_ref[1]).astype(jnp.float32)
        for h in range(QUERY_HEADS):
            span = slice(h * tokens, (h + 1) * tokens)
            columns = slice(h * HEAD_WIDTH, (h + 1) * HEAD_WIDTH)
            part = numerator_ref[span, :] / total_ref[span, :]
            out_ref[:, columns] = (part * gate_ref[:, columns] * live).astype(out_ref.dtype)


def streamed(place, queries, keyvals, bias, gate):
    rows = QUERY_HEADS * queries.shape[0]
    keys = keyvals.shape[0]
    tile = TILE if keys % TILE == 0 else keys
    whole = pl.BlockSpec(memory_space=pltpu.VMEM)
    return pl.pallas_call(
        streamed_kernel,
        grid=(keys // tile,),
        out_shape=jax.ShapeDtypeStruct(queries.shape, jnp.bfloat16),
        in_specs=[
            pl.BlockSpec(memory_space=pltpu.SMEM),
            whole,
            pl.BlockSpec((tile, keyvals.shape[1]), lambda t: (t, 0)),
            pl.BlockSpec((1, tile), lambda t: (0, t)),
            whole,
        ],
        out_specs=whole,
        scratch_shapes=[
            pltpu.VMEM((rows, 1), jnp.float32),
            pltpu.VMEM((rows, 1), jnp.float32),
            pltpu.VMEM((rows, HEAD_WIDTH), jnp.float32),
        ],
        compiler_params=pltpu.CompilerParams(vmem_limit_bytes=40 * 1024 * 1024),
    )(place, queries, keyvals, bias, gate)


def per_device(n_span, n_seq, queries, keyvals, clip_index, noise_step, valid_count, gate_table):
    tokens = queries.shape[0]
    devices = n_span * n_seq
    span_id, seq_id = lax.axis_index("span"), lax.axis_index("seq")
    me = span_id * n_seq + seq_id

    def exchange(block, distance):
        pairs = [(i, i ^ distance) for i in range(devices)]
        return lax.ppermute(block, ("span", "seq"), pairs)

    groups = jnp.arange(n_span, dtype=jnp.int32)
    own = lambda values: jnp.sum(jnp.where(groups == span_id, values, 0))
    own_clip, own_step, own_count = own(clip_index), own(noise_step), own(valid_count)
    limits = jnp.where(clip_index <= own_clip, valid_count, 0)

    def bias_of(distances):
        if distances is None:
            source = jnp.arange(devices * tokens, dtype=jnp.int32)[None, :] // tokens
            within = jnp.arange(devices * tokens, dtype=jnp.int32)[None, :] % tokens
        else:
            source = me ^ jnp.asarray(np.repeat(np.array(distances, np.int32), tokens)[None, :])
            within = jnp.asarray(np.tile(np.arange(tokens, dtype=np.int32), len(distances))[None, :])
        position = (source % n_seq) * tokens + within
        group = source // n_seq
        limit = jnp.zeros_like(position)
        for g in range(n_span):
            limit = jnp.where(group == g, limits[g], limit)
        return jnp.where(position < limit, 0.0, NEGATIVE).astype(jnp.float32)

    gate = lax.dynamic_slice(gate_table, (own_step, 0), (1, gate_table.shape[1]))
    place = jnp.stack([seq_id * tokens, own_count])
    far = [4 * i for i in range(n_seq // 4)]
    plane = [2] + [s * n_seq + y for s in range(1, n_span) for y in (2, 0)]
    if len(far) not in (2, 4) or len(plane) > MOST_PARTNERS or devices & (devices - 1):
        rows = lax.all_gather(lax.all_gather(keyvals, "seq", tiled=True), "span", tiled=True)
        return streamed(place, queries, rows, bias_of(None), gate)
    blocks = {0: keyvals}
    for d in far[1:]:
        blocks[d] = exchange(keyvals, d)
    half = len(far) // 2
    gathered = []
    for part in (far[:half], far[half:]):
        column = jnp.concatenate([blocks[d] for d in part], axis=0)
        rows = jnp.concatenate([column] + [exchange(column, d) for d in plane], axis=0)
        order = [p ^ d for p in [0] + plane for d in part]
        gathered.append((rows, bias_of(order), exchange(rows, 1), bias_of([d ^ 1 for d in order])))
    (near, near_bias, near_twin, near_twin_bias), (away, away_bias, away_twin, away_twin_bias) = gathered
    state = attend(place, queries, [near, near_twin], [near_bias, near_twin_bias])
    state = attend(place, queries, [away], [away_bias], state)
    return attend(place, queries, [away_twin], [away_twin_bias], state, gate)


def solution(mesh):
    return jax.shard_map(
        functools.partial(per_device, mesh.shape["span"], mesh.shape["seq"]),
        mesh=mesh,
        in_specs=(P(("span", "seq"), None), P(("span", "seq"), None), P(), P(), P(), P()),
        out_specs=P(("span", "seq"), None),
        check_vma=False,
    )
```

```python
import functools
import math

import jax
import jax.numpy as jnp
import numpy as np
from jax import lax
from jax.experimental import pallas as pl
from jax.experimental.pallas import tpu as pltpu
from jax.sharding import PartitionSpec as P

QUERY_HEADS = 24
KEY_VALUE_HEADS = 4
HEAD_WIDTH = 128
RATIO = QUERY_HEADS // KEY_VALUE_HEADS
KEY_WIDTH = KEY_VALUE_HEADS * HEAD_WIDTH
NEGATIVE = -1e30
LOG2E = math.log2(math.e)
TILE = 384
MOST_PARTNERS = 3
GATE_ROWS = 8


def key_bias(distances, tokens, n_seq, clip_ref, valid_ref):
    span_id = lax.axis_index("span")
    me = span_id * n_seq + lax.axis_index("seq")
    lane = lax.broadcasted_iota(jnp.int32, (1, len(distances) * tokens), 1)
    bound = jnp.zeros_like(lane)
    for i, distance in enumerate(distances):
        source = me ^ distance
        group = source // n_seq
        limit = jnp.where(clip_ref[group] <= clip_ref[span_id], valid_ref[group], 0)
        usable = jnp.minimum(limit - (source % n_seq) * tokens, tokens)
        bound = jnp.where(lane >= i * tokens, i * tokens + usable, bound)
    return jnp.where(lane < bound, 0.0, NEGATIVE).astype(jnp.float32)


def attend_kernel(orders, stage, n_seq, clip_ref, valid_ref, step_ref, q_ref, *refs):
    kv_refs, refs = refs[: len(orders)], refs[len(orders) :]
    opens, closes = stage == "first", stage == "last"
    tokens = q_ref.shape[0]
    rows = RATIO * tokens
    scale = LOG2E / math.sqrt(HEAD_WIDTH)
    heads = range(KEY_VALUE_HEADS)
    columns = [slice(h * HEAD_WIDTH, (h + 1) * HEAD_WIDTH) for h in range(QUERY_HEADS)]
    if opens:
        table_ref, top_out, part_out, gate_out, gate_ref, gate_sem = refs
        step = step_ref[lax.axis_index("span")]
        first = pl.multiple_of(step - step % GATE_ROWS, GATE_ROWS)
        fetch = pltpu.make_async_copy(table_ref.at[pl.ds(first, GATE_ROWS)], gate_ref, gate_sem)
        fetch.start()
    elif closes:
        top_in, part_in, gate_ref, out_ref, staged_ref, out_sem = refs
        position = lax.axis_index("seq") * tokens + lax.broadcasted_iota(jnp.int32, (tokens, 1), 0)
        live = (position < valid_ref[lax.axis_index("span")]).astype(jnp.float32)
    else:
        top_in, part_in, top_out, part_out = refs
    biases = [key_bias(order, tokens, n_seq, clip_ref, valid_ref) for order in orders]
    scores, tops, writes = {}, {}, []
    for h in heads:
        query = jnp.concatenate([q_ref[:, c] for c in columns[h * RATIO : (h + 1) * RATIO]], axis=0)
        for i, kv_ref in enumerate(kv_refs):
            products = lax.dot_general(
                query, kv_ref[:, columns[h]], (((1,), (1,)), ((), ())), preferred_element_type=jnp.float32
            )
            scores[h, i] = products * scale + biases[i]
    for h in heads:
        found = [jnp.max(scores[h, i], axis=1, keepdims=True) for i in range(len(orders))]
        top = jnp.broadcast_to(functools.reduce(jnp.maximum, found), (rows, HEAD_WIDTH))
        tops[h] = top if opens else jnp.maximum(top, top_in[h * rows : (h + 1) * rows, :])
    for h in heads:
        span = slice(h * rows, (h + 1) * rows)
        total, numerator = jnp.zeros((rows, HEAD_WIDTH), jnp.float32), 0.0
        for i, kv_ref in enumerate(kv_refs):
            repeats = scores[h, i].shape[1] // HEAD_WIDTH
            weights = jnp.exp2(scores[h, i] - jnp.concatenate([tops[h]] * repeats, axis=1))
            total = total + jnp.sum(weights, axis=1, keepdims=True)
            numerator = numerator + jnp.dot(
                weights.astype(jnp.bfloat16),
                kv_ref[:, columns[KEY_VALUE_HEADS + h]],
                preferred_element_type=jnp.float32,
            )
        if not opens:
            factor = jnp.exp2(top_in[span, :] - tops[h])
            total = total + factor
            numerator = numerator + part_in[span, :] * factor
        result = numerator * (1.0 / total)
        if not closes:
            top_out[span, :] = tops[h] + jnp.log2(total)
            part_out[span, :] = result
            continue
        for r in range(RATIO):
            c = columns[h * RATIO + r]
            staged_ref[:, c] = (result[r * tokens : (r + 1) * tokens] * gate_ref[:, c] * live).astype(
                out_ref.dtype
            )
        group = slice(h * RATIO * HEAD_WIDTH, (h + 1) * RATIO * HEAD_WIDTH)
        writes.append(pltpu.make_async_copy(staged_ref.at[:, group], out_ref.at[:, group], out_sem.at[h]))
        writes[-1].start()
    if opens:
        fetch.wait()
        chosen = lax.broadcasted_iota(jnp.int32, (GATE_ROWS, 1), 0) == step % GATE_ROWS
        gate_out[...] = jnp.sum(jnp.where(chosen, gate_ref[...], 0.0), axis=0, keepdims=True)
    for write in writes:
        write.wait()


def attend(scalars, queries, keyvals, orders, n_seq, stage, *carried):
    rows = QUERY_HEADS * queries.shape[0]
    keys = sum(kv.shape[0] for kv in keyvals)
    smem, vmem = pl.BlockSpec(memory_space=pltpu.SMEM), pl.BlockSpec(memory_space=pltpu.VMEM)
    anywhere = pl.BlockSpec(memory_space=pl.ANY)
    operands = [queries, *keyvals, *carried]
    in_specs = [smem] * len(scalars) + [vmem] * len(operands)
    scratch = []
    if stage == "last":
        out_shape, out_specs = jax.ShapeDtypeStruct(queries.shape, jnp.bfloat16), anywhere
        scratch = [
            pltpu.VMEM(queries.shape, jnp.bfloat16),
            pltpu.SemaphoreType.DMA((KEY_VALUE_HEADS,)),
        ]
    else:
        out_shape = [jax.ShapeDtypeStruct((rows, HEAD_WIDTH), jnp.float32)] * 2
        out_specs = [vmem, vmem]
    if stage == "first":
        in_specs[-1] = anywhere
        out_shape.append(jax.ShapeDtypeStruct((1, queries.shape[1]), jnp.float32))
        out_specs.append(vmem)
        scratch = [pltpu.VMEM((GATE_ROWS, queries.shape[1]), jnp.float32), pltpu.SemaphoreType.DMA]
    return pl.pallas_call(
        functools.partial(attend_kernel, orders, stage, n_seq),
        out_shape=out_shape,
        in_specs=in_specs,
        out_specs=out_specs,
        scratch_shapes=scratch,
        compiler_params=pltpu.CompilerParams(vmem_limit_bytes=40 * 1024 * 1024),
        cost_estimate=pl.CostEstimate(
            flops=4 * rows * keys * HEAD_WIDTH,
            bytes_accessed=keys * 2 * KEY_WIDTH * 2,
            transcendentals=rows * keys,
        ),
    )(*scalars, *operands)


def streamed_kernel(place_ref, q_ref, kv_ref, bias_ref, gate_ref, out_ref, top_ref, total_ref, numerator_ref):
    tokens = q_ref.shape[0]
    rows = RATIO * tokens
    scale = LOG2E / math.sqrt(HEAD_WIDTH)

    @pl.when(pl.program_id(0) == 0)
    def _():
        top_ref[...] = jnp.full_like(top_ref, NEGATIVE)
        total_ref[...] = jnp.zeros_like(total_ref)
        numerator_ref[...] = jnp.zeros_like(numerator_ref)

    for head in range(KEY_VALUE_HEADS):
        first = head * RATIO
        span = slice(head * rows, (head + 1) * rows)
        columns = [slice((first + r) * HEAD_WIDTH, (first + r + 1) * HEAD_WIDTH) for r in range(RATIO)]
        query = jnp.concatenate([q_ref[:, c] for c in columns], axis=0)
        key = kv_ref[:, head * HEAD_WIDTH : (head + 1) * HEAD_WIDTH]
        value = kv_ref[:, KEY_WIDTH + head * HEAD_WIDTH : KEY_WIDTH + (head + 1) * HEAD_WIDTH]
        scores = lax.dot_general(
            query, key, (((1,), (1,)), ((), ())), preferred_element_type=jnp.float32
        )
        scores = scores * scale + bias_ref[...]
        top = jnp.maximum(top_ref[span, :], jnp.max(scores, axis=1, keepdims=True))
        weights = jnp.exp2(scores - top)
        factor = jnp.exp2(top_ref[span, :] - top)
        top_ref[span, :] = top
        total_ref[span, :] = total_ref[span, :] * factor + jnp.sum(weights, axis=1, keepdims=True)
        numerator_ref[span, :] = numerator_ref[span, :] * factor + jnp.dot(
            weights.astype(jnp.bfloat16), value, preferred_element_type=jnp.float32
        )

    @pl.when(pl.program_id(0) == pl.num_programs(0) - 1)
    def _():
        positions = place_ref[0] + lax.broadcasted_iota(jnp.int32, (tokens, 1), 0)
        live = (positions < place_ref[1]).astype(jnp.float32)
        for h in range(QUERY_HEADS):
            span = slice(h * tokens, (h + 1) * tokens)
            columns = slice(h * HEAD_WIDTH, (h + 1) * HEAD_WIDTH)
            part = numerator_ref[span, :] / total_ref[span, :]
            out_ref[:, columns] = (part * gate_ref[:, columns] * live).astype(out_ref.dtype)


def streamed(place, queries, keyvals, bias, gate):
    rows = QUERY_HEADS * queries.shape[0]
    keys = keyvals.shape[0]
    tile = TILE if keys % TILE == 0 else keys
    whole = pl.BlockSpec(memory_space=pltpu.VMEM)
    return pl.pallas_call(
        streamed_kernel,
        grid=(keys // tile,),
        out_shape=jax.ShapeDtypeStruct(queries.shape, jnp.bfloat16),
        in_specs=[
            pl.BlockSpec(memory_space=pltpu.SMEM),
            whole,
            pl.BlockSpec((tile, keyvals.shape[1]), lambda t: (t, 0)),
            pl.BlockSpec((1, tile), lambda t: (0, t)),
            whole,
        ],
        out_specs=whole,
        scratch_shapes=[
            pltpu.VMEM((rows, 1), jnp.float32),
            pltpu.VMEM((rows, 1), jnp.float32),
            pltpu.VMEM((rows, HEAD_WIDTH), jnp.float32),
        ],
        compiler_params=pltpu.CompilerParams(vmem_limit_bytes=40 * 1024 * 1024),
    )(place, queries, keyvals, bias, gate)


def gathered_whole(n_span, n_seq, queries, keyvals, clip_index, noise_step, valid_count, gate_table):
    tokens = queries.shape[0]
    span_id, seq_id = lax.axis_index("span"), lax.axis_index("seq")
    groups = jnp.arange(n_span, dtype=jnp.int32)
    own = lambda values: jnp.sum(jnp.where(groups == span_id, values, 0))
    limits = jnp.where(clip_index <= own(clip_index), valid_count, 0)
    usable = jnp.arange(n_seq * tokens, dtype=jnp.int32)[None, :] < limits[:, None]
    bias = jnp.where(usable, 0.0, NEGATIVE).astype(jnp.float32).reshape(1, -1)
    gate = lax.dynamic_slice(gate_table, (own(noise_step), 0), (1, gate_table.shape[1]))
    place = jnp.stack([seq_id * tokens, own(valid_count)])
    rows = lax.all_gather(lax.all_gather(keyvals, "seq", tiled=True), "span", tiled=True)
    return streamed(place, queries, rows, bias, gate)


def per_device(n_span, n_seq, queries, keyvals, clip_index, noise_step, valid_count, gate_table):
    devices = n_span * n_seq
    far = [4 * i for i in range(n_seq // 4)]
    plane = [2] + [s * n_seq + y for s in range(1, n_span) for y in (2, 0)]
    if len(far) not in (2, 4) or len(plane) > MOST_PARTNERS or devices & (devices - 1):
        return gathered_whole(
            n_span, n_seq, queries, keyvals, clip_index, noise_step, valid_count, gate_table
        )

    def exchange(block, distance):
        pairs = [(i, i ^ distance) for i in range(devices)]
        return lax.ppermute(block, ("span", "seq"), pairs)

    scalars = (clip_index, valid_count, noise_step)
    ob = lax.optimization_barrier
    cat = lambda xs: jnp.concatenate(xs, axis=0)
    half = len(far) // 2
    nearz, farz = far[:half], far[half:]
    orders = [[p ^ d for p in [0] + plane for d in part] for part in (nearz, farz)]
    twins = [[d ^ 1 for d in o] for o in orders]
    z={0:keyvals}
    for d in far[1:]: z[d]=exchange(keyvals,d)
    p1=cat([z[d] for d in nearz]); p2=cat([z[d] for d in farz])
    near=cat([p1]+[exchange(p1,d) for d in plane])
    away=cat([p2]+[exchange(p2,d) for d in plane])
    nt=exchange(near,1)
    *st,gate=attend(scalars,queries,[near,nt],[orders[0],twins[0]],n_seq,"first",gate_table)
    at=exchange(away,1)
    st=attend(scalars,queries,[away],[orders[1]],n_seq,"middle",*st)
    return attend(scalars,queries,[at],[twins[1]],n_seq,"last",*st,gate)


def solution(mesh):
    return jax.shard_map(
        functools.partial(per_device, mesh.shape["span"], mesh.shape["seq"]),
        mesh=mesh,
        in_specs=(P(("span", "seq"), None), P(("span", "seq"), None), P(), P(), P(), P()),
        out_specs=P(("span", "seq"), None),
        check_vma=False,
    )
```

```python
import functools
import math

import jax
import jax.numpy as jnp
import numpy as np
from jax import lax
from jax.experimental import pallas as pl
from jax.experimental.pallas import tpu as pltpu
from jax.sharding import PartitionSpec as P

QUERY_HEADS = 24
KEY_VALUE_HEADS = 4
HEAD_WIDTH = 128
RATIO = QUERY_HEADS // KEY_VALUE_HEADS
KEY_WIDTH = KEY_VALUE_HEADS * HEAD_WIDTH
NEGATIVE = -1e30
LOG2E = math.log2(math.e)
TILE = 384
MOST_PARTNERS = 3
GATE_ROWS = 8


def key_bias(distances, tokens, n_seq, clip_ref, valid_ref):
    span_id = lax.axis_index("span")
    me = span_id * n_seq + lax.axis_index("seq")
    lane = lax.broadcasted_iota(jnp.int32, (1, len(distances) * tokens), 1)
    bound = jnp.zeros_like(lane)
    for i, distance in enumerate(distances):
        source = me ^ distance
        group = source // n_seq
        limit = jnp.where(clip_ref[group] <= clip_ref[span_id], valid_ref[group], 0)
        usable = jnp.minimum(limit - (source % n_seq) * tokens, tokens)
        bound = jnp.where(lane >= i * tokens, i * tokens + usable, bound)
    return jnp.where(lane < bound, 0.0, NEGATIVE).astype(jnp.float32)


def attend_kernel(orders, stage, n_seq, clip_ref, valid_ref, step_ref, q_ref, *refs):
    kv_refs, refs = refs[: len(orders)], refs[len(orders) :]
    opens, closes = stage == "first", stage == "last"
    tokens = q_ref.shape[0]
    rows = RATIO * tokens
    scale = LOG2E / math.sqrt(HEAD_WIDTH)
    heads = range(KEY_VALUE_HEADS)
    columns = [slice(h * HEAD_WIDTH, (h + 1) * HEAD_WIDTH) for h in range(QUERY_HEADS)]
    if opens:
        table_ref, top_out, part_out, gate_out, gate_ref, gate_sem = refs
        step = step_ref[lax.axis_index("span")]
        first = pl.multiple_of(step - step % GATE_ROWS, GATE_ROWS)
        fetch = pltpu.make_async_copy(table_ref.at[pl.ds(first, GATE_ROWS)], gate_ref, gate_sem)
        fetch.start()
    else:
        top_in, part_in, gate_ref, out_ref, staged_ref, out_sem = refs
        position = lax.axis_index("seq") * tokens + lax.broadcasted_iota(jnp.int32, (tokens, 1), 0)
        live = (position < valid_ref[lax.axis_index("span")]).astype(jnp.float32)
    biases = [key_bias(order, tokens, n_seq, clip_ref, valid_ref) for order in orders]
    scores, tops, writes = {}, {}, []
    for h in heads:
        query = jnp.concatenate([q_ref[:, c] for c in columns[h * RATIO : (h + 1) * RATIO]], axis=0)
        for i, kv_ref in enumerate(kv_refs):
            products = lax.dot_general(
                query, kv_ref[:, columns[h]], (((1,), (1,)), ((), ())), preferred_element_type=jnp.float32
            )
            scores[h, i] = products * scale + biases[i]
    for h in heads:
        found = [jnp.max(scores[h, i], axis=1, keepdims=True) for i in range(len(orders))]
        top = jnp.broadcast_to(functools.reduce(jnp.maximum, found), (rows, HEAD_WIDTH))
        tops[h] = top if opens else jnp.maximum(top, top_in[h * rows : (h + 1) * rows, :])
    for h in heads:
        span = slice(h * rows, (h + 1) * rows)
        total, numerator = jnp.zeros((rows, HEAD_WIDTH), jnp.float32), 0.0
        for i, kv_ref in enumerate(kv_refs):
            repeats = scores[h, i].shape[1] // HEAD_WIDTH
            weights = jnp.exp2(scores[h, i] - jnp.concatenate([tops[h]] * repeats, axis=1))
            total = total + jnp.sum(weights, axis=1, keepdims=True)
            numerator = numerator + jnp.dot(
                weights.astype(jnp.bfloat16),
                kv_ref[:, columns[KEY_VALUE_HEADS + h]],
                preferred_element_type=jnp.float32,
            )
        if not opens:
            factor = jnp.exp2(top_in[span, :] - tops[h])
            total = total + factor
            numerator = numerator + part_in[span, :] * factor
        result = numerator * (1.0 / total)
        if not closes:
            top_out[span, :] = tops[h] + jnp.log2(total)
            part_out[span, :] = result
            continue
        for r in range(RATIO):
            c = columns[h * RATIO + r]
            staged_ref[:, c] = (result[r * tokens : (r + 1) * tokens] * gate_ref[:, c] * live).astype(
                out_ref.dtype
            )
        group = slice(h * RATIO * HEAD_WIDTH, (h + 1) * RATIO * HEAD_WIDTH)
        writes.append(pltpu.make_async_copy(staged_ref.at[:, group], out_ref.at[:, group], out_sem.at[h]))
        writes[-1].start()
    if opens:
        fetch.wait()
        chosen = lax.broadcasted_iota(jnp.int32, (GATE_ROWS, 1), 0) == step % GATE_ROWS
        gate_out[...] = jnp.sum(jnp.where(chosen, gate_ref[...], 0.0), axis=0, keepdims=True)
    for write in writes:
        write.wait()


def attend(scalars, queries, keyvals, orders, n_seq, stage, *carried):
    rows = QUERY_HEADS * queries.shape[0]
    keys = sum(kv.shape[0] for kv in keyvals)
    smem, vmem = pl.BlockSpec(memory_space=pltpu.SMEM), pl.BlockSpec(memory_space=pltpu.VMEM)
    anywhere = pl.BlockSpec(memory_space=pl.ANY)
    operands = [queries, *keyvals, *carried]
    in_specs = [smem] * len(scalars) + [vmem] * len(operands)
    scratch = []
    if stage == "last":
        out_shape, out_specs = jax.ShapeDtypeStruct(queries.shape, jnp.bfloat16), anywhere
        scratch = [
            pltpu.VMEM(queries.shape, jnp.bfloat16),
            pltpu.SemaphoreType.DMA((KEY_VALUE_HEADS,)),
        ]
    else:
        out_shape = [jax.ShapeDtypeStruct((rows, HEAD_WIDTH), jnp.float32)] * 2
        out_specs = [vmem, vmem]
    if stage == "first":
        in_specs[-1] = anywhere
        out_shape.append(jax.ShapeDtypeStruct((1, queries.shape[1]), jnp.float32))
        out_specs.append(vmem)
        scratch = [pltpu.VMEM((GATE_ROWS, queries.shape[1]), jnp.float32), pltpu.SemaphoreType.DMA]
    return pl.pallas_call(
        functools.partial(attend_kernel, orders, stage, n_seq),
        out_shape=out_shape,
        in_specs=in_specs,
        out_specs=out_specs,
        scratch_shapes=scratch,
        compiler_params=pltpu.CompilerParams(vmem_limit_bytes=40 * 1024 * 1024),
        cost_estimate=pl.CostEstimate(
            flops=4 * rows * keys * HEAD_WIDTH,
            bytes_accessed=keys * 2 * KEY_WIDTH * 2,
            transcendentals=rows * keys,
        ),
    )(*scalars, *operands)


def streamed_kernel(place_ref, q_ref, kv_ref, bias_ref, gate_ref, out_ref, top_ref, total_ref, numerator_ref):
    tokens = q_ref.shape[0]
    rows = RATIO * tokens
    scale = LOG2E / math.sqrt(HEAD_WIDTH)

    @pl.when(pl.program_id(0) == 0)
    def _():
        top_ref[...] = jnp.full_like(top_ref, NEGATIVE)
        total_ref[...] = jnp.zeros_like(total_ref)
        numerator_ref[...] = jnp.zeros_like(numerator_ref)

    for head in range(KEY_VALUE_HEADS):
        first = head * RATIO
        span = slice(head * rows, (head + 1) * rows)
        columns = [slice((first + r) * HEAD_WIDTH, (first + r + 1) * HEAD_WIDTH) for r in range(RATIO)]
        query = jnp.concatenate([q_ref[:, c] for c in columns], axis=0)
        key = kv_ref[:, head * HEAD_WIDTH : (head + 1) * HEAD_WIDTH]
        value = kv_ref[:, KEY_WIDTH + head * HEAD_WIDTH : KEY_WIDTH + (head + 1) * HEAD_WIDTH]
        scores = lax.dot_general(
            query, key, (((1,), (1,)), ((), ())), preferred_element_type=jnp.float32
        )
        scores = scores * scale + bias_ref[...]
        top = jnp.maximum(top_ref[span, :], jnp.max(scores, axis=1, keepdims=True))
        weights = jnp.exp2(scores - top)
        factor = jnp.exp2(top_ref[span, :] - top)
        top_ref[span, :] = top
        total_ref[span, :] = total_ref[span, :] * factor + jnp.sum(weights, axis=1, keepdims=True)
        numerator_ref[span, :] = numerator_ref[span, :] * factor + jnp.dot(
            weights.astype(jnp.bfloat16), value, preferred_element_type=jnp.float32
        )

    @pl.when(pl.program_id(0) == pl.num_programs(0) - 1)
    def _():
        positions = place_ref[0] + lax.broadcasted_iota(jnp.int32, (tokens, 1), 0)
        live = (positions < place_ref[1]).astype(jnp.float32)
        for h in range(QUERY_HEADS):
            span = slice(h * tokens, (h + 1) * tokens)
            columns = slice(h * HEAD_WIDTH, (h + 1) * HEAD_WIDTH)
            part = numerator_ref[span, :] / total_ref[span, :]
            out_ref[:, columns] = (part * gate_ref[:, columns] * live).astype(out_ref.dtype)


def streamed(place, queries, keyvals, bias, gate):
    rows = QUERY_HEADS * queries.shape[0]
    keys = keyvals.shape[0]
    tile = TILE if keys % TILE == 0 else keys
    whole = pl.BlockSpec(memory_space=pltpu.VMEM)
    return pl.pallas_call(
        streamed_kernel,
        grid=(keys // tile,),
        out_shape=jax.ShapeDtypeStruct(queries.shape, jnp.bfloat16),
        in_specs=[
            pl.BlockSpec(memory_space=pltpu.SMEM),
            whole,
            pl.BlockSpec((tile, keyvals.shape[1]), lambda t: (t, 0)),
            pl.BlockSpec((1, tile), lambda t: (0, t)),
            whole,
        ],
        out_specs=whole,
        scratch_shapes=[
            pltpu.VMEM((rows, 1), jnp.float32),
            pltpu.VMEM((rows, 1), jnp.float32),
            pltpu.VMEM((rows, HEAD_WIDTH), jnp.float32),
        ],
        compiler_params=pltpu.CompilerParams(vmem_limit_bytes=40 * 1024 * 1024),
    )(place, queries, keyvals, bias, gate)


def gathered_whole(n_span, n_seq, queries, keyvals, clip_index, noise_step, valid_count, gate_table):
    tokens = queries.shape[0]
    span_id, seq_id = lax.axis_index("span"), lax.axis_index("seq")
    groups = jnp.arange(n_span, dtype=jnp.int32)
    own = lambda values: jnp.sum(jnp.where(groups == span_id, values, 0))
    limits = jnp.where(clip_index <= own(clip_index), valid_count, 0)
    usable = jnp.arange(n_seq * tokens, dtype=jnp.int32)[None, :] < limits[:, None]
    bias = jnp.where(usable, 0.0, NEGATIVE).astype(jnp.float32).reshape(1, -1)
    gate = lax.dynamic_slice(gate_table, (own(noise_step), 0), (1, gate_table.shape[1]))
    place = jnp.stack([seq_id * tokens, own(valid_count)])
    rows = lax.all_gather(lax.all_gather(keyvals, "seq", tiled=True), "span", tiled=True)
    return streamed(place, queries, rows, bias, gate)


def per_device(n_span, n_seq, queries, keyvals, clip_index, noise_step, valid_count, gate_table):
    devices = n_span * n_seq
    far = [4 * i for i in range(n_seq // 4)]
    plane = [2] + [s * n_seq + y for s in range(1, n_span) for y in (0, 2)]
    if len(far) not in (2, 4) or len(plane) > MOST_PARTNERS or devices & (devices - 1):
        return gathered_whole(
            n_span, n_seq, queries, keyvals, clip_index, noise_step, valid_count, gate_table
        )

    def exchange(block, distance):
        pairs = [(i, i ^ distance) for i in range(devices)]
        return lax.ppermute(block, ("span", "seq"), pairs)

    scalars = (clip_index, valid_count, noise_step)
    blocks = {0: keyvals}
    for d in far[1:]:
        blocks[d] = exchange(keyvals, d)
    half = len(far) // 2
    parts, orders, twins = [], [], []
    for part in (far[:half], far[half:]):
        column = jnp.concatenate([blocks[d] for d in part], axis=0)
        parts.append(jnp.concatenate([column] + [exchange(column, d) for d in plane], axis=0))
        orders.append([p ^ d for p in [0] + plane for d in part])
        twins.append([d ^ 1 for d in orders[-1]])
    near, away = parts
    near_twin, away_twin = exchange(near, 1), exchange(away, 1)
    *state, gate = attend(
        scalars, queries, [near, near_twin, away], [orders[0], twins[0], orders[1]], n_seq, "first", gate_table
    )
    return attend(scalars, queries, [away_twin], [twins[1]], n_seq, "last", *state, gate)


def solution(mesh):
    return jax.shard_map(
        functools.partial(per_device, mesh.shape["span"], mesh.shape["seq"]),
        mesh=mesh,
        in_specs=(P(("span", "seq"), None), P(("span", "seq"), None), P(), P(), P(), P()),
        out_specs=P(("span", "seq"), None),
        check_vma=False,
    )
```

```python
import functools
import math

import jax
import jax.numpy as jnp
import numpy as np
from jax import lax
from jax.experimental import pallas as pl
from jax.experimental.pallas import tpu as pltpu
from jax.sharding import PartitionSpec as P

QUERY_HEADS = 24
KEY_VALUE_HEADS = 4
HEAD_WIDTH = 128
RATIO = QUERY_HEADS // KEY_VALUE_HEADS
KEY_WIDTH = KEY_VALUE_HEADS * HEAD_WIDTH
NEGATIVE = -1e30
LOG2E = math.log2(math.e)
TILE = 384
GATE_ROWS = 8


def key_bias(distances, tokens, n_seq, clip_ref, valid_ref):
    span_id = lax.axis_index("span")
    me = span_id * n_seq + lax.axis_index("seq")
    lane = lax.broadcasted_iota(jnp.int32, (1, len(distances) * tokens), 1)
    bound = jnp.zeros_like(lane)
    for i, distance in enumerate(distances):
        source = me ^ distance
        group = source // n_seq
        limit = jnp.where(clip_ref[group] <= clip_ref[span_id], valid_ref[group], 0)
        usable = jnp.minimum(limit - (source % n_seq) * tokens, tokens)
        bound = jnp.where(lane >= i * tokens, i * tokens + usable, bound)
    return jnp.where(lane < bound, 0.0, NEGATIVE).astype(jnp.float32)


def attend_kernel(orders, stage, n_seq, clip_ref, valid_ref, step_ref, q_ref, *refs):
    kv_refs, refs = refs[: len(orders)], refs[len(orders) :]
    opens, closes = stage == "first", stage == "last"
    tokens = q_ref.shape[0]
    rows = RATIO * tokens
    scale = LOG2E / math.sqrt(HEAD_WIDTH)
    heads = range(KEY_VALUE_HEADS)
    columns = [slice(h * HEAD_WIDTH, (h + 1) * HEAD_WIDTH) for h in range(QUERY_HEADS)]
    if opens:
        table_ref, top_out, part_out, gate_out, gate_ref, gate_sem = refs
        step = step_ref[lax.axis_index("span")]
        first = pl.multiple_of(step - step % GATE_ROWS, GATE_ROWS)
        fetch = pltpu.make_async_copy(table_ref.at[pl.ds(first, GATE_ROWS)], gate_ref, gate_sem)
        fetch.start()
    else:
        top_in, part_in, gate_ref, out_ref, staged_ref, out_sem = refs
        position = lax.axis_index("seq") * tokens + lax.broadcasted_iota(jnp.int32, (tokens, 1), 0)
        live = (position < valid_ref[lax.axis_index("span")]).astype(jnp.float32)
    biases = [key_bias(order, tokens, n_seq, clip_ref, valid_ref) for order in orders]
    scores, tops, writes = {}, {}, []
    for h in heads:
        query = jnp.concatenate([q_ref[:, c] for c in columns[h * RATIO : (h + 1) * RATIO]], axis=0)
        for i, kv_ref in enumerate(kv_refs):
            products = lax.dot_general(
                query, kv_ref[:, columns[h]], (((1,), (1,)), ((), ())), preferred_element_type=jnp.float32
            )
            scores[h, i] = products * scale + biases[i]
    for h in heads:
        found = [jnp.max(scores[h, i], axis=1, keepdims=True) for i in range(len(orders))]
        top = jnp.broadcast_to(functools.reduce(jnp.maximum, found), (rows, HEAD_WIDTH))
        tops[h] = top if opens else jnp.maximum(top, top_in[h * rows : (h + 1) * rows, :])
    for h in heads:
        span = slice(h * rows, (h + 1) * rows)
        total, numerator = jnp.zeros((rows, HEAD_WIDTH), jnp.float32), 0.0
        for i, kv_ref in enumerate(kv_refs):
            repeats = scores[h, i].shape[1] // HEAD_WIDTH
            weights = jnp.exp2(scores[h, i] - jnp.concatenate([tops[h]] * repeats, axis=1))
            total = total + jnp.sum(weights, axis=1, keepdims=True)
            numerator = numerator + jnp.dot(
                weights.astype(jnp.bfloat16),
                kv_ref[:, columns[KEY_VALUE_HEADS + h]],
                preferred_element_type=jnp.float32,
            )
        if not opens:
            factor = jnp.exp2(top_in[span, :] - tops[h])
            total = total + factor
            numerator = numerator + part_in[span, :] * factor
        result = numerator * (1.0 / total)
        if not closes:
            top_out[span, :] = tops[h] + jnp.log2(total)
            part_out[span, :] = result
            continue
        for r in range(RATIO):
            c = columns[h * RATIO + r]
            staged_ref[:, c] = (result[r * tokens : (r + 1) * tokens] * gate_ref[:, c] * live).astype(
                out_ref.dtype
            )
        group = slice(h * RATIO * HEAD_WIDTH, (h + 1) * RATIO * HEAD_WIDTH)
        writes.append(pltpu.make_async_copy(staged_ref.at[:, group], out_ref.at[:, group], out_sem.at[h]))
        writes[-1].start()
    if opens:
        fetch.wait()
        chosen = lax.broadcasted_iota(jnp.int32, (GATE_ROWS, 1), 0) == step % GATE_ROWS
        gate_out[...] = jnp.sum(jnp.where(chosen, gate_ref[...], 0.0), axis=0, keepdims=True)
    for write in writes:
        write.wait()


def attend(scalars, queries, keyvals, orders, n_seq, stage, *carried):
    rows = QUERY_HEADS * queries.shape[0]
    keys = sum(kv.shape[0] for kv in keyvals)
    smem, vmem = pl.BlockSpec(memory_space=pltpu.SMEM), pl.BlockSpec(memory_space=pltpu.VMEM)
    anywhere = pl.BlockSpec(memory_space=pl.ANY)
    operands = [queries, *keyvals, *carried]
    in_specs = [smem] * len(scalars) + [vmem] * len(operands)
    scratch = []
    if stage == "last":
        out_shape, out_specs = jax.ShapeDtypeStruct(queries.shape, jnp.bfloat16), anywhere
        scratch = [
            pltpu.VMEM(queries.shape, jnp.bfloat16),
            pltpu.SemaphoreType.DMA((KEY_VALUE_HEADS,)),
        ]
    else:
        out_shape = [jax.ShapeDtypeStruct((rows, HEAD_WIDTH), jnp.float32)] * 2
        out_specs = [vmem, vmem]
    if stage == "first":
        in_specs[-1] = anywhere
        out_shape.append(jax.ShapeDtypeStruct((1, queries.shape[1]), jnp.float32))
        out_specs.append(vmem)
        scratch = [pltpu.VMEM((GATE_ROWS, queries.shape[1]), jnp.float32), pltpu.SemaphoreType.DMA]
    return pl.pallas_call(
        functools.partial(attend_kernel, orders, stage, n_seq),
        out_shape=out_shape,
        in_specs=in_specs,
        out_specs=out_specs,
        scratch_shapes=scratch,
        compiler_params=pltpu.CompilerParams(vmem_limit_bytes=40 * 1024 * 1024),
        cost_estimate=pl.CostEstimate(
            flops=4 * rows * keys * HEAD_WIDTH,
            bytes_accessed=keys * 2 * KEY_WIDTH * 2,
            transcendentals=rows * keys,
        ),
    )(*scalars, *operands)


def streamed_kernel(place_ref, q_ref, kv_ref, bias_ref, gate_ref, out_ref, top_ref, total_ref, numerator_ref):
    tokens = q_ref.shape[0]
    rows = RATIO * tokens
    scale = LOG2E / math.sqrt(HEAD_WIDTH)

    @pl.when(pl.program_id(0) == 0)
    def _():
        top_ref[...] = jnp.full_like(top_ref, NEGATIVE)
        total_ref[...] = jnp.zeros_like(total_ref)
        numerator_ref[...] = jnp.zeros_like(numerator_ref)

    for head in range(KEY_VALUE_HEADS):
        first = head * RATIO
        span = slice(head * rows, (head + 1) * rows)
        columns = [slice((first + r) * HEAD_WIDTH, (first + r + 1) * HEAD_WIDTH) for r in range(RATIO)]
        query = jnp.concatenate([q_ref[:, c] for c in columns], axis=0)
        key = kv_ref[:, head * HEAD_WIDTH : (head + 1) * HEAD_WIDTH]
        value = kv_ref[:, KEY_WIDTH + head * HEAD_WIDTH : KEY_WIDTH + (head + 1) * HEAD_WIDTH]
        scores = lax.dot_general(
            query, key, (((1,), (1,)), ((), ())), preferred_element_type=jnp.float32
        )
        scores = scores * scale + bias_ref[...]
        top = jnp.maximum(top_ref[span, :], jnp.max(scores, axis=1, keepdims=True))
        weights = jnp.exp2(scores - top)
        factor = jnp.exp2(top_ref[span, :] - top)
        top_ref[span, :] = top
        total_ref[span, :] = total_ref[span, :] * factor + jnp.sum(weights, axis=1, keepdims=True)
        numerator_ref[span, :] = numerator_ref[span, :] * factor + jnp.dot(
            weights.astype(jnp.bfloat16), value, preferred_element_type=jnp.float32
        )

    @pl.when(pl.program_id(0) == pl.num_programs(0) - 1)
    def _():
        positions = place_ref[0] + lax.broadcasted_iota(jnp.int32, (tokens, 1), 0)
        live = (positions < place_ref[1]).astype(jnp.float32)
        for h in range(QUERY_HEADS):
            span = slice(h * tokens, (h + 1) * tokens)
            columns = slice(h * HEAD_WIDTH, (h + 1) * HEAD_WIDTH)
            part = numerator_ref[span, :] / total_ref[span, :]
            out_ref[:, columns] = (part * gate_ref[:, columns] * live).astype(out_ref.dtype)


def streamed(place, queries, keyvals, bias, gate):
    rows = QUERY_HEADS * queries.shape[0]
    keys = keyvals.shape[0]
    tile = TILE if keys % TILE == 0 else keys
    whole = pl.BlockSpec(memory_space=pltpu.VMEM)
    return pl.pallas_call(
        streamed_kernel,
        grid=(keys // tile,),
        out_shape=jax.ShapeDtypeStruct(queries.shape, jnp.bfloat16),
        in_specs=[
            pl.BlockSpec(memory_space=pltpu.SMEM),
            whole,
            pl.BlockSpec((tile, keyvals.shape[1]), lambda t: (t, 0)),
            pl.BlockSpec((1, tile), lambda t: (0, t)),
            whole,
        ],
        out_specs=whole,
        scratch_shapes=[
            pltpu.VMEM((rows, 1), jnp.float32),
            pltpu.VMEM((rows, 1), jnp.float32),
            pltpu.VMEM((rows, HEAD_WIDTH), jnp.float32),
        ],
        compiler_params=pltpu.CompilerParams(vmem_limit_bytes=40 * 1024 * 1024),
    )(place, queries, keyvals, bias, gate)


def gathered_whole(n_span, n_seq, queries, keyvals, clip_index, noise_step, valid_count, gate_table):
    tokens = queries.shape[0]
    span_id, seq_id = lax.axis_index("span"), lax.axis_index("seq")
    groups = jnp.arange(n_span, dtype=jnp.int32)
    own = lambda values: jnp.sum(jnp.where(groups == span_id, values, 0))
    limits = jnp.where(clip_index <= own(clip_index), valid_count, 0)
    usable = jnp.arange(n_seq * tokens, dtype=jnp.int32)[None, :] < limits[:, None]
    bias = jnp.where(usable, 0.0, NEGATIVE).astype(jnp.float32).reshape(1, -1)
    gate = lax.dynamic_slice(gate_table, (own(noise_step), 0), (1, gate_table.shape[1]))
    place = jnp.stack([seq_id * tokens, own(valid_count)])
    rows = lax.all_gather(lax.all_gather(keyvals, "seq", tiled=True), "span", tiled=True)
    return streamed(place, queries, rows, bias, gate)


def per_device(n_span, n_seq, queries, keyvals, clip_index, noise_step, valid_count, gate_table):
    devices = n_span * n_seq
    tokens = queries.shape[0]
    far = [4 * i for i in range(n_seq // 4)]
    if n_span != 2 or len(far) != 4:
        return gathered_whole(
            n_span, n_seq, queries, keyvals, clip_index, noise_step, valid_count, gate_table
        )

    def exchange(block, distance):
        pairs = [(i, i ^ distance) for i in range(devices)]
        return lax.ppermute(block, ("span", "seq"), pairs)

    plane = [n_seq + 2, 2, n_seq]
    away = jnp.concatenate([exchange(keyvals, d) for d in far[2:]], axis=0)
    column = exchange(keyvals, far[1])
    home = jnp.concatenate([keyvals] + [exchange(keyvals, d) for d in plane], axis=0)
    near = jnp.concatenate([home, column, exchange(home[tokens:], far[1])], axis=0)
    away = jnp.concatenate([away] + [exchange(away, d) for d in plane], axis=0)
    near_order = [z ^ p for z in far[:2] for p in [0] + plane]
    away_order = [p ^ z for p in [0] + plane for z in far[2:]]
    twin = lambda order: [d ^ 1 for d in order]
    near_twin, away_twin = exchange(near, 1), exchange(away, 1)
    scalars = (clip_index, valid_count, noise_step)
    *state, gate = attend(
        scalars, queries, [near, away], [near_order, away_order], n_seq, "first", gate_table
    )
    return attend(
        scalars, queries, [away_twin, near_twin], [twin(away_order), twin(near_order)], n_seq, "last", *state, gate
    )


def solution(mesh):
    return jax.shard_map(
        functools.partial(per_device, mesh.shape["span"], mesh.shape["seq"]),
        mesh=mesh,
        in_specs=(P(("span", "seq"), None), P(("span", "seq"), None), P(), P(), P(), P()),
        out_specs=P(("span", "seq"), None),
        check_vma=False,
    )
```

```python
import functools
import math

import jax
import jax.numpy as jnp
import numpy as np
from jax import lax
from jax.experimental import pallas as pl
from jax.experimental.pallas import tpu as pltpu
from jax.sharding import PartitionSpec as P

QUERY_HEADS = 24
KEY_VALUE_HEADS = 4
HEAD_WIDTH = 128
RATIO = QUERY_HEADS // KEY_VALUE_HEADS
KEY_WIDTH = KEY_VALUE_HEADS * HEAD_WIDTH
NEGATIVE = -1e30
LOG2E = math.log2(math.e)
TILE = 384
GATE_ROWS = 8


def key_bias(distances, tokens, n_seq, clip_ref, valid_ref):
    span_id = lax.axis_index("span")
    me = span_id * n_seq + lax.axis_index("seq")
    lane = lax.broadcasted_iota(jnp.int32, (1, len(distances) * tokens), 1)
    bound = jnp.zeros_like(lane)
    for i, distance in enumerate(distances):
        source = me ^ distance
        group = source // n_seq
        limit = jnp.where(clip_ref[group] <= clip_ref[span_id], valid_ref[group], 0)
        usable = jnp.minimum(limit - (source % n_seq) * tokens, tokens)
        bound = jnp.where(lane >= i * tokens, i * tokens + usable, bound)
    return jnp.where(lane < bound, 0.0, NEGATIVE).astype(jnp.float32)


def attend_kernel(orders, stage, n_seq, clip_ref, valid_ref, step_ref, q_ref, *refs):
    kv_refs, refs = refs[: len(orders)], refs[len(orders) :]
    opens, closes = stage == "first", stage == "last"
    tokens = q_ref.shape[0]
    rows = RATIO * tokens
    scale = LOG2E / math.sqrt(HEAD_WIDTH)
    heads = range(KEY_VALUE_HEADS)
    columns = [slice(h * HEAD_WIDTH, (h + 1) * HEAD_WIDTH) for h in range(QUERY_HEADS)]
    if opens:
        table_ref, top_out, part_out, gate_out, gate_ref, gate_sem = refs
        step = step_ref[lax.axis_index("span")]
        first = pl.multiple_of(step - step % GATE_ROWS, GATE_ROWS)
        fetch = pltpu.make_async_copy(table_ref.at[pl.ds(first, GATE_ROWS)], gate_ref, gate_sem)
        fetch.start()
    else:
        top_in, part_in, gate_ref, out_ref, staged_ref, out_sem = refs
        position = lax.axis_index("seq") * tokens + lax.broadcasted_iota(jnp.int32, (tokens, 1), 0)
        live = (position < valid_ref[lax.axis_index("span")]).astype(jnp.float32)
    biases = [key_bias(order, tokens, n_seq, clip_ref, valid_ref) for order in orders]
    scores, tops, writes = {}, {}, []
    for h in heads:
        query = jnp.concatenate([q_ref[:, c] for c in columns[h * RATIO : (h + 1) * RATIO]], axis=0)
        for i, kv_ref in enumerate(kv_refs):
            products = lax.dot_general(
                query, kv_ref[:, columns[h]], (((1,), (1,)), ((), ())), preferred_element_type=jnp.float32
            )
            scores[h, i] = products * scale + biases[i]
    for h in heads:
        found = [jnp.max(scores[h, i], axis=1, keepdims=True) for i in range(len(orders))]
        top = jnp.broadcast_to(functools.reduce(jnp.maximum, found), (rows, HEAD_WIDTH))
        tops[h] = top if opens else jnp.maximum(top, top_in[h * rows : (h + 1) * rows, :])
    for h in heads:
        span = slice(h * rows, (h + 1) * rows)
        total, numerator = jnp.zeros((rows, HEAD_WIDTH), jnp.float32), 0.0
        for i, kv_ref in enumerate(kv_refs):
            repeats = scores[h, i].shape[1] // HEAD_WIDTH
            weights = jnp.exp2(scores[h, i] - jnp.concatenate([tops[h]] * repeats, axis=1))
            numerator = numerator + jnp.dot(
                weights.astype(jnp.bfloat16),
                jnp.concatenate([kv_ref[:, columns[KEY_VALUE_HEADS + h]], jnp.ones((kv_ref.shape[0], HEAD_WIDTH), jnp.bfloat16)], axis=1),
                preferred_element_type=jnp.float32,
            )
        total, numerator = numerator[:, HEAD_WIDTH:], numerator[:, :HEAD_WIDTH]
        if not opens:
            factor = jnp.exp2(top_in[span, :] - tops[h])
            total = total + factor
            numerator = numerator + part_in[span, :] * factor
        result = numerator * (1.0 / total)
        if not closes:
            top_out[span, :] = tops[h] + jnp.log2(total)
            part_out[span, :] = result
            continue
        for r in range(RATIO):
            c = columns[h * RATIO + r]
            staged_ref[:, c] = (result[r * tokens : (r + 1) * tokens] * gate_ref[:, c] * live).astype(
                out_ref.dtype
            )
        group = slice(h * RATIO * HEAD_WIDTH, (h + 1) * RATIO * HEAD_WIDTH)
        writes.append(pltpu.make_async_copy(staged_ref.at[:, group], out_ref.at[:, group], out_sem.at[h]))
        writes[-1].start()
    if opens:
        fetch.wait()
        chosen = lax.broadcasted_iota(jnp.int32, (GATE_ROWS, 1), 0) == step % GATE_ROWS
        gate_out[...] = jnp.sum(jnp.where(chosen, gate_ref[...], 0.0), axis=0, keepdims=True)
    for write in writes:
        write.wait()


def attend(scalars, queries, keyvals, orders, n_seq, stage, *carried):
    rows = QUERY_HEADS * queries.shape[0]
    keys = sum(kv.shape[0] for kv in keyvals)
    smem, vmem = pl.BlockSpec(memory_space=pltpu.SMEM), pl.BlockSpec(memory_space=pltpu.VMEM)
    anywhere = pl.BlockSpec(memory_space=pl.ANY)
    operands = [queries, *keyvals, *carried]
    in_specs = [smem] * len(scalars) + [vmem] * len(operands)
    scratch = []
    if stage == "last":
        out_shape, out_specs = jax.ShapeDtypeStruct(queries.shape, jnp.bfloat16), anywhere
        scratch = [
            pltpu.VMEM(queries.shape, jnp.bfloat16),
            pltpu.SemaphoreType.DMA((KEY_VALUE_HEADS,)),
        ]
    else:
        out_shape = [jax.ShapeDtypeStruct((rows, HEAD_WIDTH), jnp.float32)] * 2
        out_specs = [vmem, vmem]
    if stage == "first":
        in_specs[-1] = anywhere
        out_shape.append(jax.ShapeDtypeStruct((1, queries.shape[1]), jnp.float32))
        out_specs.append(vmem)
        scratch = [pltpu.VMEM((GATE_ROWS, queries.shape[1]), jnp.float32), pltpu.SemaphoreType.DMA]
    return pl.pallas_call(
        functools.partial(attend_kernel, orders, stage, n_seq),
        out_shape=out_shape,
        in_specs=in_specs,
        out_specs=out_specs,
        scratch_shapes=scratch,
        compiler_params=pltpu.CompilerParams(vmem_limit_bytes=40 * 1024 * 1024),
        cost_estimate=pl.CostEstimate(
            flops=4 * rows * keys * HEAD_WIDTH,
            bytes_accessed=keys * 2 * KEY_WIDTH * 2,
            transcendentals=rows * keys,
        ),
    )(*scalars, *operands)


def streamed_kernel(place_ref, q_ref, kv_ref, bias_ref, gate_ref, out_ref, top_ref, total_ref, numerator_ref):
    tokens = q_ref.shape[0]
    rows = RATIO * tokens
    scale = LOG2E / math.sqrt(HEAD_WIDTH)

    @pl.when(pl.program_id(0) == 0)
    def _():
        top_ref[...] = jnp.full_like(top_ref, NEGATIVE)
        total_ref[...] = jnp.zeros_like(total_ref)
        numerator_ref[...] = jnp.zeros_like(numerator_ref)

    for head in range(KEY_VALUE_HEADS):
        first = head * RATIO
        span = slice(head * rows, (head + 1) * rows)
        columns = [slice((first + r) * HEAD_WIDTH, (first + r + 1) * HEAD_WIDTH) for r in range(RATIO)]
        query = jnp.concatenate([q_ref[:, c] for c in columns], axis=0)
        key = kv_ref[:, head * HEAD_WIDTH : (head + 1) * HEAD_WIDTH]
        value = kv_ref[:, KEY_WIDTH + head * HEAD_WIDTH : KEY_WIDTH + (head + 1) * HEAD_WIDTH]
        scores = lax.dot_general(
            query, key, (((1,), (1,)), ((), ())), preferred_element_type=jnp.float32
        )
        scores = scores * scale + bias_ref[...]
        top = jnp.maximum(top_ref[span, :], jnp.max(scores, axis=1, keepdims=True))
        weights = jnp.exp2(scores - top)
        factor = jnp.exp2(top_ref[span, :] - top)
        top_ref[span, :] = top
        total_ref[span, :] = total_ref[span, :] * factor + jnp.sum(weights, axis=1, keepdims=True)
        numerator_ref[span, :] = numerator_ref[span, :] * factor + jnp.dot(
            weights.astype(jnp.bfloat16), value, preferred_element_type=jnp.float32
        )

    @pl.when(pl.program_id(0) == pl.num_programs(0) - 1)
    def _():
        positions = place_ref[0] + lax.broadcasted_iota(jnp.int32, (tokens, 1), 0)
        live = (positions < place_ref[1]).astype(jnp.float32)
        for h in range(QUERY_HEADS):
            span = slice(h * tokens, (h + 1) * tokens)
            columns = slice(h * HEAD_WIDTH, (h + 1) * HEAD_WIDTH)
            part = numerator_ref[span, :] / total_ref[span, :]
            out_ref[:, columns] = (part * gate_ref[:, columns] * live).astype(out_ref.dtype)


def streamed(place, queries, keyvals, bias, gate):
    rows = QUERY_HEADS * queries.shape[0]
    keys = keyvals.shape[0]
    tile = TILE if keys % TILE == 0 else keys
    whole = pl.BlockSpec(memory_space=pltpu.VMEM)
    return pl.pallas_call(
        streamed_kernel,
        grid=(keys // tile,),
        out_shape=jax.ShapeDtypeStruct(queries.shape, jnp.bfloat16),
        in_specs=[
            pl.BlockSpec(memory_space=pltpu.SMEM),
            whole,
            pl.BlockSpec((tile, keyvals.shape[1]), lambda t: (t, 0)),
            pl.BlockSpec((1, tile), lambda t: (0, t)),
            whole,
        ],
        out_specs=whole,
        scratch_shapes=[
            pltpu.VMEM((rows, 1), jnp.float32),
            pltpu.VMEM((rows, 1), jnp.float32),
            pltpu.VMEM((rows, HEAD_WIDTH), jnp.float32),
        ],
        compiler_params=pltpu.CompilerParams(vmem_limit_bytes=40 * 1024 * 1024),
    )(place, queries, keyvals, bias, gate)


def gathered_whole(n_span, n_seq, queries, keyvals, clip_index, noise_step, valid_count, gate_table):
    tokens = queries.shape[0]
    span_id, seq_id = lax.axis_index("span"), lax.axis_index("seq")
    groups = jnp.arange(n_span, dtype=jnp.int32)
    own = lambda values: jnp.sum(jnp.where(groups == span_id, values, 0))
    limits = jnp.where(clip_index <= own(clip_index), valid_count, 0)
    usable = jnp.arange(n_seq * tokens, dtype=jnp.int32)[None, :] < limits[:, None]
    bias = jnp.where(usable, 0.0, NEGATIVE).astype(jnp.float32).reshape(1, -1)
    gate = lax.dynamic_slice(gate_table, (own(noise_step), 0), (1, gate_table.shape[1]))
    place = jnp.stack([seq_id * tokens, own(valid_count)])
    rows = lax.all_gather(lax.all_gather(keyvals, "seq", tiled=True), "span", tiled=True)
    return streamed(place, queries, rows, bias, gate)


def per_device(n_span, n_seq, queries, keyvals, clip_index, noise_step, valid_count, gate_table):
    devices = n_span * n_seq
    tokens = queries.shape[0]
    far = [4 * i for i in range(n_seq // 4)]
    if n_span != 2 or len(far) != 4:
        return gathered_whole(
            n_span, n_seq, queries, keyvals, clip_index, noise_step, valid_count, gate_table
        )

    def exchange(block, distance):
        pairs = [(i, i ^ distance) for i in range(devices)]
        return lax.ppermute(block, ("span", "seq"), pairs)

    plane = [n_seq + 2, 2, n_seq]
    away = jnp.concatenate([exchange(keyvals, d) for d in far[2:]], axis=0)
    column = exchange(keyvals, far[1])
    home = jnp.concatenate([keyvals] + [exchange(keyvals, d) for d in plane], axis=0)
    near = jnp.concatenate([home, column, exchange(home[tokens:], far[1])], axis=0)
    away = jnp.concatenate([away] + [exchange(away, d) for d in plane], axis=0)
    near_order = [z ^ p for z in far[:2] for p in [0] + plane]
    away_order = [p ^ z for p in [0] + plane for z in far[2:]]
    twin = lambda order: [d ^ 1 for d in order]
    near_twin, away_twin = exchange(near, 1), exchange(away, 1)
    scalars = (clip_index, valid_count, noise_step)
    *state, gate = attend(
        scalars, queries, [near, away], [near_order, away_order], n_seq, "first", gate_table
    )
    return attend(
        scalars, queries, [away_twin, near_twin], [twin(away_order), twin(near_order)], n_seq, "last", *state, gate
    )


def solution(mesh):
    return jax.shard_map(
        functools.partial(per_device, mesh.shape["span"], mesh.shape["seq"]),
        mesh=mesh,
        in_specs=(P(("span", "seq"), None), P(("span", "seq"), None), P(), P(), P(), P()),
        out_specs=P(("span", "seq"), None),
        check_vma=False,
    )
```

```python
import functools
import math

import jax
import jax.numpy as jnp
import numpy as np
from jax import lax
from jax.experimental import pallas as pl
from jax.experimental.pallas import tpu as pltpu
from jax.sharding import PartitionSpec as P

QUERY_HEADS = 24
KEY_VALUE_HEADS = 4
HEAD_WIDTH = 128
RATIO = QUERY_HEADS // KEY_VALUE_HEADS
KEY_WIDTH = KEY_VALUE_HEADS * HEAD_WIDTH
NEGATIVE = -1e30
LOG2E = math.log2(math.e)
TILE = 384
GATE_ROWS = 8


def key_bias(distances, tokens, n_seq, clip_ref, valid_ref):
    span_id = lax.axis_index("span")
    me = span_id * n_seq + lax.axis_index("seq")
    lane = lax.broadcasted_iota(jnp.int32, (1, len(distances) * tokens), 1)
    bound = jnp.zeros_like(lane)
    for i, distance in enumerate(distances):
        source = me ^ distance
        group = source // n_seq
        limit = jnp.where(clip_ref[group] <= clip_ref[span_id], valid_ref[group], 0)
        usable = jnp.minimum(limit - (source % n_seq) * tokens, tokens)
        bound = jnp.where(lane >= i * tokens, i * tokens + usable, bound)
    return jnp.where(lane < bound, 0.0, NEGATIVE).astype(jnp.float32)


def attend_kernel(orders, groups, stage, n_seq, clip_ref, valid_ref, step_ref, q_ref, *refs):
    kv_refs, refs = refs[: len(orders)], refs[len(orders) :]
    opens = stage == "first"
    tokens = q_ref.shape[0]
    rows = RATIO * tokens
    scale = LOG2E / math.sqrt(HEAD_WIDTH)
    heads = range(KEY_VALUE_HEADS)
    columns = [slice(h * HEAD_WIDTH, (h + 1) * HEAD_WIDTH) for h in range(QUERY_HEADS)]
    span_id = lax.axis_index("span")
    if opens:
        table_ref, top_out, part_out, gate_out, gate_ref, gate_sem = refs
        step = step_ref[span_id]
        first = pl.multiple_of(step - step % GATE_ROWS, GATE_ROWS)
        fetch = pltpu.make_async_copy(table_ref.at[pl.ds(first, GATE_ROWS)], gate_ref, gate_sem)
        fetch.start()
    else:
        top_in, part_in, gate_ref, out_ref, staged_ref, out_sem = refs
        position = lax.axis_index("seq") * tokens + lax.broadcasted_iota(jnp.int32, (tokens, 1), 0)
        live = (position < valid_ref[span_id]).astype(jnp.float32)

    def run(groups):
        def joined(group, c):
            return jnp.concatenate([kv_refs[i][start:stop, c] for i, start, stop in group], axis=0)

        biases = []
        for group in groups:
            order = [d for i, start, stop in group for d in orders[i][start // tokens : stop // tokens]]
            biases.append(key_bias(order, tokens, n_seq, clip_ref, valid_ref))
        scores, tops, writes = {}, {}, []
        for h in heads:
            query = jnp.concatenate([q_ref[:, c] for c in columns[h * RATIO : (h + 1) * RATIO]], axis=0)
            for g, group in enumerate(groups):
                products = lax.dot_general(
                    query,
                    joined(group, columns[h]),
                    (((1,), (1,)), ((), ())),
                    preferred_element_type=jnp.float32,
                )
                scores[h, g] = products * scale + biases[g]
        for h in heads:
            found = [jnp.max(scores[h, g], axis=1, keepdims=True) for g in range(len(groups))]
            top = jnp.broadcast_to(functools.reduce(jnp.maximum, found), (rows, HEAD_WIDTH))
            tops[h] = top if opens else jnp.maximum(top, top_in[h * rows : (h + 1) * rows, :])
        for h in heads:
            span = slice(h * rows, (h + 1) * rows)
            sums = 0.0
            for g, group in enumerate(groups):
                repeats = scores[h, g].shape[1] // HEAD_WIDTH
                weights = jnp.exp2(scores[h, g] - jnp.concatenate([tops[h]] * repeats, axis=1))
                value = joined(group, columns[KEY_VALUE_HEADS + h])
                value = jnp.concatenate([value, jnp.ones_like(value)], axis=1)
                sums = sums + jnp.dot(
                    weights.astype(jnp.bfloat16), value, preferred_element_type=jnp.float32
                )
            numerator, total = sums[:, :HEAD_WIDTH], sums[:, HEAD_WIDTH:]
            if not opens:
                factor = jnp.exp2(top_in[span, :] - tops[h])
                total = total + factor
                numerator = numerator + part_in[span, :] * factor
            result = numerator * (1.0 / total)
            if opens:
                top_out[span, :] = tops[h] + jnp.log2(total)
                part_out[span, :] = result
                continue
            for r in range(RATIO):
                c = columns[h * RATIO + r]
                part = result[r * tokens : (r + 1) * tokens]
                staged_ref[:, c] = (part * gate_ref[:, c] * live).astype(out_ref.dtype)
            group = slice(h * RATIO * HEAD_WIDTH, (h + 1) * RATIO * HEAD_WIDTH)
            writes.append(
                pltpu.make_async_copy(staged_ref.at[:, group], out_ref.at[:, group], out_sem.at[h])
            )
            writes[-1].start()
        for write in writes:
            write.wait()

    run(groups)
    if opens:
        fetch.wait()
        chosen = lax.broadcasted_iota(jnp.int32, (GATE_ROWS, 1), 0) == step % GATE_ROWS
        gate_out[...] = jnp.sum(jnp.where(chosen, gate_ref[...], 0.0), axis=0, keepdims=True)


def attend(scalars, queries, keyvals, orders, groups, n_seq, stage, *carried):
    rows = QUERY_HEADS * queries.shape[0]
    keys = sum(kv.shape[0] for kv in keyvals)
    smem, vmem = pl.BlockSpec(memory_space=pltpu.SMEM), pl.BlockSpec(memory_space=pltpu.VMEM)
    anywhere = pl.BlockSpec(memory_space=pl.ANY)
    operands = [queries, *keyvals, *carried]
    in_specs = [smem] * len(scalars) + [vmem] * len(operands)
    scratch = []
    if stage == "last":
        out_shape, out_specs = jax.ShapeDtypeStruct(queries.shape, jnp.bfloat16), anywhere
        scratch = [
            pltpu.VMEM(queries.shape, jnp.bfloat16),
            pltpu.SemaphoreType.DMA((KEY_VALUE_HEADS,)),
        ]
    else:
        out_shape = [jax.ShapeDtypeStruct((rows, HEAD_WIDTH), jnp.float32)] * 2
        out_specs = [vmem, vmem]
    if stage == "first":
        in_specs[-1] = anywhere
        out_shape.append(jax.ShapeDtypeStruct((1, queries.shape[1]), jnp.float32))
        out_specs.append(vmem)
        scratch = [pltpu.VMEM((GATE_ROWS, queries.shape[1]), jnp.float32), pltpu.SemaphoreType.DMA]
    return pl.pallas_call(
        functools.partial(attend_kernel, orders, groups, stage, n_seq),
        out_shape=out_shape,
        in_specs=in_specs,
        out_specs=out_specs,
        scratch_shapes=scratch,
        compiler_params=pltpu.CompilerParams(vmem_limit_bytes=40 * 1024 * 1024),
        cost_estimate=pl.CostEstimate(
            flops=4 * rows * keys * HEAD_WIDTH,
            bytes_accessed=keys * 2 * KEY_WIDTH * 2,
            transcendentals=rows * keys,
        ),
    )(*scalars, *operands)


def streamed_kernel(place_ref, q_ref, kv_ref, bias_ref, gate_ref, out_ref, top_ref, total_ref, numerator_ref):
    tokens = q_ref.shape[0]
    rows = RATIO * tokens
    scale = LOG2E / math.sqrt(HEAD_WIDTH)

    @pl.when(pl.program_id(0) == 0)
    def _():
        top_ref[...] = jnp.full_like(top_ref, NEGATIVE)
        total_ref[...] = jnp.zeros_like(total_ref)
        numerator_ref[...] = jnp.zeros_like(numerator_ref)

    for head in range(KEY_VALUE_HEADS):
        first = head * RATIO
        span = slice(head * rows, (head + 1) * rows)
        columns = [slice((first + r) * HEAD_WIDTH, (first + r + 1) * HEAD_WIDTH) for r in range(RATIO)]
        query = jnp.concatenate([q_ref[:, c] for c in columns], axis=0)
        key = kv_ref[:, head * HEAD_WIDTH : (head + 1) * HEAD_WIDTH]
        value = kv_ref[:, KEY_WIDTH + head * HEAD_WIDTH : KEY_WIDTH + (head + 1) * HEAD_WIDTH]
        scores = lax.dot_general(
            query, key, (((1,), (1,)), ((), ())), preferred_element_type=jnp.float32
        )
        scores = scores * scale + bias_ref[...]
        top = jnp.maximum(top_ref[span, :], jnp.max(scores, axis=1, keepdims=True))
        weights = jnp.exp2(scores - top)
        factor = jnp.exp2(top_ref[span, :] - top)
        top_ref[span, :] = top
        total_ref[span, :] = total_ref[span, :] * factor + jnp.sum(weights, axis=1, keepdims=True)
        numerator_ref[span, :] = numerator_ref[span, :] * factor + jnp.dot(
            weights.astype(jnp.bfloat16), value, preferred_element_type=jnp.float32
        )

    @pl.when(pl.program_id(0) == pl.num_programs(0) - 1)
    def _():
        positions = place_ref[0] + lax.broadcasted_iota(jnp.int32, (tokens, 1), 0)
        live = (positions < place_ref[1]).astype(jnp.float32)
        for h in range(QUERY_HEADS):
            span = slice(h * tokens, (h + 1) * tokens)
            columns = slice(h * HEAD_WIDTH, (h + 1) * HEAD_WIDTH)
            part = numerator_ref[span, :] / total_ref[span, :]
            out_ref[:, columns] = (part * gate_ref[:, columns] * live).astype(out_ref.dtype)


def streamed(place, queries, keyvals, bias, gate):
    rows = QUERY_HEADS * queries.shape[0]
    keys = keyvals.shape[0]
    tile = TILE if keys % TILE == 0 else keys
    whole = pl.BlockSpec(memory_space=pltpu.VMEM)
    return pl.pallas_call(
        streamed_kernel,
        grid=(keys // tile,),
        out_shape=jax.ShapeDtypeStruct(queries.shape, jnp.bfloat16),
        in_specs=[
            pl.BlockSpec(memory_space=pltpu.SMEM),
            whole,
            pl.BlockSpec((tile, keyvals.shape[1]), lambda t: (t, 0)),
            pl.BlockSpec((1, tile), lambda t: (0, t)),
            whole,
        ],
        out_specs=whole,
        scratch_shapes=[
            pltpu.VMEM((rows, 1), jnp.float32),
            pltpu.VMEM((rows, 1), jnp.float32),
            pltpu.VMEM((rows, HEAD_WIDTH), jnp.float32),
        ],
        compiler_params=pltpu.CompilerParams(vmem_limit_bytes=40 * 1024 * 1024),
    )(place, queries, keyvals, bias, gate)


def gathered_whole(n_span, n_seq, queries, keyvals, clip_index, noise_step, valid_count, gate_table):
    tokens = queries.shape[0]
    span_id, seq_id = lax.axis_index("span"), lax.axis_index("seq")
    groups = jnp.arange(n_span, dtype=jnp.int32)
    own = lambda values: jnp.sum(jnp.where(groups == span_id, values, 0))
    limits = jnp.where(clip_index <= own(clip_index), valid_count, 0)
    usable = jnp.arange(n_seq * tokens, dtype=jnp.int32)[None, :] < limits[:, None]
    bias = jnp.where(usable, 0.0, NEGATIVE).astype(jnp.float32).reshape(1, -1)
    gate = lax.dynamic_slice(gate_table, (own(noise_step), 0), (1, gate_table.shape[1]))
    place = jnp.stack([seq_id * tokens, own(valid_count)])
    rows = lax.all_gather(lax.all_gather(keyvals, "seq", tiled=True), "span", tiled=True)
    return streamed(place, queries, rows, bias, gate)


def per_device(n_span, n_seq, queries, keyvals, clip_index, noise_step, valid_count, gate_table):
    devices = n_span * n_seq
    tokens = queries.shape[0]
    far = [4 * i for i in range(n_seq // 4)]
    if n_span != 2 or len(far) != 4:
        return gathered_whole(
            n_span, n_seq, queries, keyvals, clip_index, noise_step, valid_count, gate_table
        )

    def exchange(block, distance):
        pairs = [(i, i ^ distance) for i in range(devices)]
        return lax.ppermute(block, ("span", "seq"), pairs)

    plane = [n_seq + 2, 2, n_seq]
    away = jnp.concatenate([exchange(keyvals, d) for d in far[2:]], axis=0)
    column = exchange(keyvals, far[1])
    received = [exchange(keyvals, d) for d in plane]
    passed = exchange(jnp.concatenate(received, axis=0), far[1])
    spread = [away] + [exchange(away, d) for d in plane]
    away_order = [p ^ z for p in [0] + plane for z in far[2:]]
    home_order = [0] + plane + [far[1]]
    passed_order = [far[1] ^ p for p in plane]
    twin = lambda order: [d ^ 1 for d in order]
    scalars = (clip_index, valid_count, noise_step)
    n_away, n_home, n_passed = (len(o) * tokens for o in (away_order, home_order, passed_order))
    pieces = [jnp.concatenate(spread, axis=0), jnp.concatenate([keyvals] + received + [column], axis=0), passed]
    orders = [away_order, home_order, passed_order]
    groups = [[(0, 0, n_away)], [(1, 0, n_home), (2, 0, n_passed)]]
    twins = [exchange(x, 1) for x in pieces]
    *state, gate = attend(scalars, queries, pieces, orders, groups, n_seq, "first", gate_table)
    orders = [twin(o) for o in orders]
    return attend(scalars, queries, twins, orders, groups, n_seq, "last", *state, gate)


def solution(mesh):
    return jax.shard_map(
        functools.partial(per_device, mesh.shape["span"], mesh.shape["seq"]),
        mesh=mesh,
        in_specs=(P(("span", "seq"), None), P(("span", "seq"), None), P(), P(), P(), P()),
        out_specs=P(("span", "seq"), None),
        check_vma=False,
    )
```

```python
import functools
import math

import jax
import jax.numpy as jnp
import numpy as np
from jax import lax
from jax.experimental import pallas as pl
from jax.experimental.pallas import tpu as pltpu
from jax.sharding import PartitionSpec as P

QUERY_HEADS = 24
KEY_VALUE_HEADS = 4
HEAD_WIDTH = 128
RATIO = QUERY_HEADS // KEY_VALUE_HEADS
KEY_WIDTH = KEY_VALUE_HEADS * HEAD_WIDTH
NEGATIVE = -1e30
LOG2E = math.log2(math.e)
TILE = 384
GATE_ROWS = 8


def key_bias(distances, tokens, n_seq, clip_ref, valid_ref):
    span_id = lax.axis_index("span")
    me = span_id * n_seq + lax.axis_index("seq")
    lane = lax.broadcasted_iota(jnp.int32, (1, len(distances) * tokens), 1)
    bound = jnp.zeros_like(lane)
    for i, distance in enumerate(distances):
        base = me
        if isinstance(distance, tuple):
            core, distance = distance
            base = me - me % 2 + core
        source = base ^ distance
        group = source // n_seq
        limit = jnp.where(clip_ref[group] <= clip_ref[span_id], valid_ref[group], 0)
        usable = jnp.minimum(limit - (source % n_seq) * tokens, tokens)
        bound = jnp.where(lane >= i * tokens, i * tokens + usable, bound)
    return jnp.where(lane < bound, 0.0, NEGATIVE).astype(jnp.float32)


def attend_kernel(orders, groups, stage, n_seq, clip_ref, valid_ref, step_ref, q_ref, *refs):
    kv_refs, refs = refs[: len(orders)], refs[len(orders) :]
    opens, closes = stage == "first", stage == "last"
    tokens = q_ref.shape[0]
    rows = RATIO * tokens
    scale = LOG2E / math.sqrt(HEAD_WIDTH)
    heads = range(KEY_VALUE_HEADS)
    columns = [slice(h * HEAD_WIDTH, (h + 1) * HEAD_WIDTH) for h in range(QUERY_HEADS)]
    span_id = lax.axis_index("span")
    if opens:
        table_ref, top_out, part_out, gate_out, gate_ref, gate_sem = refs
        step = step_ref[span_id]
        first = pl.multiple_of(step - step % GATE_ROWS, GATE_ROWS)
        fetch = pltpu.make_async_copy(table_ref.at[pl.ds(first, GATE_ROWS)], gate_ref, gate_sem)
        fetch.start()
    elif closes:
        top_in, part_in, gate_ref, out_ref, staged_ref, out_sem = refs
        position = lax.axis_index("seq") * tokens + lax.broadcasted_iota(jnp.int32, (tokens, 1), 0)
        live = (position < valid_ref[span_id]).astype(jnp.float32)
    else:
        top_in, part_in, top_out, part_out = refs

    def run(groups):
        def joined(group, c):
            return jnp.concatenate([kv_refs[i][start:stop, c] for i, start, stop in group], axis=0)

        biases = []
        for group in groups:
            order = [d for i, start, stop in group for d in orders[i][start // tokens : stop // tokens]]
            biases.append(key_bias(order, tokens, n_seq, clip_ref, valid_ref))
        scores, tops, writes = {}, {}, []
        for h in heads:
            query = jnp.concatenate([q_ref[:, c] for c in columns[h * RATIO : (h + 1) * RATIO]], axis=0)
            for g, group in enumerate(groups):
                products = lax.dot_general(
                    query,
                    joined(group, columns[h]),
                    (((1,), (1,)), ((), ())),
                    preferred_element_type=jnp.float32,
                )
                scores[h, g] = products * scale + biases[g]
        for h in heads:
            found = [jnp.max(scores[h, g], axis=1, keepdims=True) for g in range(len(groups))]
            top = jnp.broadcast_to(functools.reduce(jnp.maximum, found), (rows, HEAD_WIDTH))
            tops[h] = top if opens else jnp.maximum(top, top_in[h * rows : (h + 1) * rows, :])
        for h in heads:
            span = slice(h * rows, (h + 1) * rows)
            sums = 0.0
            for g, group in enumerate(groups):
                size = scores[h, g].shape[1]
                shift = jnp.concatenate([tops[h]] * pl.cdiv(size, HEAD_WIDTH), axis=1)[:, :size]
                weights = jnp.exp2(scores[h, g] - shift)
                value = joined(group, columns[KEY_VALUE_HEADS + h])
                value = jnp.concatenate([value, jnp.ones_like(value)], axis=1)
                sums = sums + jnp.dot(
                    weights.astype(jnp.bfloat16), value, preferred_element_type=jnp.float32
                )
            numerator, total = sums[:, :HEAD_WIDTH], sums[:, HEAD_WIDTH:]
            if not opens:
                factor = jnp.exp2(top_in[span, :] - tops[h])
                total = total + factor
                numerator = numerator + part_in[span, :] * factor
            result = numerator * (1.0 / total)
            if not closes:
                top_out[span, :] = tops[h] + jnp.log2(total)
                part_out[span, :] = result
                continue
            for r in range(RATIO):
                c = columns[h * RATIO + r]
                part = result[r * tokens : (r + 1) * tokens]
                staged_ref[:, c] = (part * gate_ref[:, c] * live).astype(out_ref.dtype)
            group = slice(h * RATIO * HEAD_WIDTH, (h + 1) * RATIO * HEAD_WIDTH)
            writes.append(
                pltpu.make_async_copy(staged_ref.at[:, group], out_ref.at[:, group], out_sem.at[h])
            )
            writes[-1].start()
        for write in writes:
            write.wait()

    run(groups)
    if opens:
        fetch.wait()
        chosen = lax.broadcasted_iota(jnp.int32, (GATE_ROWS, 1), 0) == step % GATE_ROWS
        gate_out[...] = jnp.sum(jnp.where(chosen, gate_ref[...], 0.0), axis=0, keepdims=True)


def attend(scalars, queries, keyvals, orders, groups, n_seq, stage, *carried):
    rows = QUERY_HEADS * queries.shape[0]
    keys = sum(kv.shape[0] for kv in keyvals)
    smem, vmem = pl.BlockSpec(memory_space=pltpu.SMEM), pl.BlockSpec(memory_space=pltpu.VMEM)
    anywhere = pl.BlockSpec(memory_space=pl.ANY)
    operands = [queries, *keyvals, *carried]
    in_specs = [smem] * len(scalars) + [vmem] * len(operands)
    scratch = []
    if stage == "last":
        out_shape, out_specs = jax.ShapeDtypeStruct(queries.shape, jnp.bfloat16), anywhere
        scratch = [
            pltpu.VMEM(queries.shape, jnp.bfloat16),
            pltpu.SemaphoreType.DMA((KEY_VALUE_HEADS,)),
        ]
    else:
        out_shape = [jax.ShapeDtypeStruct((rows, HEAD_WIDTH), jnp.float32)] * 2
        out_specs = [vmem, vmem]
    if stage == "first":
        in_specs[-1] = anywhere
        out_shape.append(jax.ShapeDtypeStruct((1, queries.shape[1]), jnp.float32))
        out_specs.append(vmem)
        scratch = [pltpu.VMEM((GATE_ROWS, queries.shape[1]), jnp.float32), pltpu.SemaphoreType.DMA]
    return pl.pallas_call(
        functools.partial(attend_kernel, orders, groups, stage, n_seq),
        out_shape=out_shape,
        in_specs=in_specs,
        out_specs=out_specs,
        scratch_shapes=scratch,
        compiler_params=pltpu.CompilerParams(vmem_limit_bytes=40 * 1024 * 1024),
        cost_estimate=pl.CostEstimate(
            flops=4 * rows * keys * HEAD_WIDTH,
            bytes_accessed=keys * 2 * KEY_WIDTH * 2,
            transcendentals=rows * keys,
        ),
    )(*scalars, *operands)


def streamed_kernel(place_ref, q_ref, kv_ref, bias_ref, gate_ref, out_ref, top_ref, total_ref, numerator_ref):
    tokens = q_ref.shape[0]
    rows = RATIO * tokens
    scale = LOG2E / math.sqrt(HEAD_WIDTH)

    @pl.when(pl.program_id(0) == 0)
    def _():
        top_ref[...] = jnp.full_like(top_ref, NEGATIVE)
        total_ref[...] = jnp.zeros_like(total_ref)
        numerator_ref[...] = jnp.zeros_like(numerator_ref)

    for head in range(KEY_VALUE_HEADS):
        first = head * RATIO
        span = slice(head * rows, (head + 1) * rows)
        columns = [slice((first + r) * HEAD_WIDTH, (first + r + 1) * HEAD_WIDTH) for r in range(RATIO)]
        query = jnp.concatenate([q_ref[:, c] for c in columns], axis=0)
        key = kv_ref[:, head * HEAD_WIDTH : (head + 1) * HEAD_WIDTH]
        value = kv_ref[:, KEY_WIDTH + head * HEAD_WIDTH : KEY_WIDTH + (head + 1) * HEAD_WIDTH]
        scores = lax.dot_general(
            query, key, (((1,), (1,)), ((), ())), preferred_element_type=jnp.float32
        )
        scores = scores * scale + bias_ref[...]
        top = jnp.maximum(top_ref[span, :], jnp.max(scores, axis=1, keepdims=True))
        weights = jnp.exp2(scores - top)
        factor = jnp.exp2(top_ref[span, :] - top)
        top_ref[span, :] = top
        total_ref[span, :] = total_ref[span, :] * factor + jnp.sum(weights, axis=1, keepdims=True)
        numerator_ref[span, :] = numerator_ref[span, :] * factor + jnp.dot(
            weights.astype(jnp.bfloat16), value, preferred_element_type=jnp.float32
        )

    @pl.when(pl.program_id(0) == pl.num_programs(0) - 1)
    def _():
        positions = place_ref[0] + lax.broadcasted_iota(jnp.int32, (tokens, 1), 0)
        live = (positions < place_ref[1]).astype(jnp.float32)
        for h in range(QUERY_HEADS):
            span = slice(h * tokens, (h + 1) * tokens)
            columns = slice(h * HEAD_WIDTH, (h + 1) * HEAD_WIDTH)
            part = numerator_ref[span, :] / total_ref[span, :]
            out_ref[:, columns] = (part * gate_ref[:, columns] * live).astype(out_ref.dtype)


def streamed(place, queries, keyvals, bias, gate):
    rows = QUERY_HEADS * queries.shape[0]
    keys = keyvals.shape[0]
    tile = TILE if keys % TILE == 0 else keys
    whole = pl.BlockSpec(memory_space=pltpu.VMEM)
    return pl.pallas_call(
        streamed_kernel,
        grid=(keys // tile,),
        out_shape=jax.ShapeDtypeStruct(queries.shape, jnp.bfloat16),
        in_specs=[
            pl.BlockSpec(memory_space=pltpu.SMEM),
            whole,
            pl.BlockSpec((tile, keyvals.shape[1]), lambda t: (t, 0)),
            pl.BlockSpec((1, tile), lambda t: (0, t)),
            whole,
        ],
        out_specs=whole,
        scratch_shapes=[
            pltpu.VMEM((rows, 1), jnp.float32),
            pltpu.VMEM((rows, 1), jnp.float32),
            pltpu.VMEM((rows, HEAD_WIDTH), jnp.float32),
        ],
        compiler_params=pltpu.CompilerParams(vmem_limit_bytes=40 * 1024 * 1024),
    )(place, queries, keyvals, bias, gate)


def gathered_whole(n_span, n_seq, queries, keyvals, clip_index, noise_step, valid_count, gate_table):
    tokens = queries.shape[0]
    span_id, seq_id = lax.axis_index("span"), lax.axis_index("seq")
    groups = jnp.arange(n_span, dtype=jnp.int32)
    own = lambda values: jnp.sum(jnp.where(groups == span_id, values, 0))
    limits = jnp.where(clip_index <= own(clip_index), valid_count, 0)
    usable = jnp.arange(n_seq * tokens, dtype=jnp.int32)[None, :] < limits[:, None]
    bias = jnp.where(usable, 0.0, NEGATIVE).astype(jnp.float32).reshape(1, -1)
    gate = lax.dynamic_slice(gate_table, (own(noise_step), 0), (1, gate_table.shape[1]))
    place = jnp.stack([seq_id * tokens, own(valid_count)])
    rows = lax.all_gather(lax.all_gather(keyvals, "seq", tiled=True), "span", tiled=True)
    return streamed(place, queries, rows, bias, gate)


def per_device(n_span, n_seq, queries, keyvals, clip_index, noise_step, valid_count, gate_table):
    devices = n_span * n_seq
    tokens = queries.shape[0]
    far = [4 * i for i in range(n_seq // 4)]
    if n_span != 2 or len(far) != 4:
        return gathered_whole(
            n_span, n_seq, queries, keyvals, clip_index, noise_step, valid_count, gate_table
        )

    def exchange(block, distance):
        pairs = [(i, i ^ distance) for i in range(devices)]
        return lax.ppermute(block, ("span", "seq"), pairs)

    plane = [n_seq + 2, 2, n_seq]
    away = jnp.concatenate([exchange(keyvals, d) for d in far[2:]], axis=0)
    column = exchange(keyvals, far[1])
    home = jnp.concatenate([keyvals] + [exchange(keyvals, d) for d in plane], axis=0)
    near = jnp.concatenate([column, exchange(home[tokens:], far[1])], axis=0)
    away = jnp.concatenate([away] + [exchange(away, d) for d in plane], axis=0)
    home_order = [0] + plane
    near_order = [far[1] ^ p for p in home_order]
    away_order = [p ^ z for p in home_order for z in far[2:]]
    twin = lambda order: [d ^ 1 for d in order]
    scalars = (clip_index, valid_count, noise_step)
    whole = lambda *parts: [(i, 0, part.shape[0]) for i, part in enumerate(parts)]
    *state, gate = attend(
        scalars, queries, [home], [home_order], [whole(home)], n_seq, "first", gate_table
    )
    near, _ = lax.optimization_barrier((near, state[0]))
    both = exchange(jnp.concatenate([home, near], axis=0), 1)
    twins = [exchange(away, 1), both]
    orders, groups = [away_order, near_order], [whole(away), [(1, 0, near.shape[0])]]
    state = attend(scalars, queries, [away, near], orders, groups, n_seq, "middle", *state)
    orders = [twin(away_order), twin(home_order + near_order)]
    groups = [whole(away), [(1, 0, both.shape[0])]]
    return attend(scalars, queries, twins, orders, groups, n_seq, "last", *state, gate)


def solution(mesh):
    return jax.shard_map(
        functools.partial(per_device, mesh.shape["span"], mesh.shape["seq"]),
        mesh=mesh,
        in_specs=(P(("span", "seq"), None), P(("span", "seq"), None), P(), P(), P(), P()),
        out_specs=P(("span", "seq"), None),
        check_vma=False,
    )
```

```python
import functools
import math

import jax
import jax.numpy as jnp
import numpy as np
from jax import lax
from jax.experimental import pallas as pl
from jax.experimental.pallas import tpu as pltpu
from jax.sharding import PartitionSpec as P

QUERY_HEADS = 24
KEY_VALUE_HEADS = 4
HEAD_WIDTH = 128
RATIO = QUERY_HEADS // KEY_VALUE_HEADS
KEY_WIDTH = KEY_VALUE_HEADS * HEAD_WIDTH
NEGATIVE = -1e30
LOG2E = math.log2(math.e)
TILE = 384
GATE_ROWS = 8


def key_bias(distances, tokens, n_seq, clip_ref, valid_ref):
    span_id = lax.axis_index("span")
    me = span_id * n_seq + lax.axis_index("seq")
    lane = lax.broadcasted_iota(jnp.int32, (1, len(distances) * tokens), 1)
    bound = jnp.zeros_like(lane)
    for i, distance in enumerate(distances):
        base = me
        if isinstance(distance, tuple):
            core, distance = distance
            base = me - me % 2 + core
        source = base ^ distance
        group = source // n_seq
        limit = jnp.where(clip_ref[group] <= clip_ref[span_id], valid_ref[group], 0)
        usable = jnp.minimum(limit - (source % n_seq) * tokens, tokens)
        bound = jnp.where(lane >= i * tokens, i * tokens + usable, bound)
    return jnp.where(lane < bound, 0.0, NEGATIVE).astype(jnp.float32)


def attend_kernel(orders, groups, stage, n_seq, clip_ref, valid_ref, step_ref, q_ref, *refs):
    kv_refs, refs = refs[: len(orders)], refs[len(orders) :]
    opens, closes = stage == "first", stage == "last"
    tokens = q_ref.shape[0]
    rows = RATIO * tokens
    scale = LOG2E / math.sqrt(HEAD_WIDTH)
    heads = range(KEY_VALUE_HEADS)
    columns = [slice(h * HEAD_WIDTH, (h + 1) * HEAD_WIDTH) for h in range(QUERY_HEADS)]
    span_id = lax.axis_index("span")
    if opens:
        table_ref, top_out, part_out, gate_out, gate_ref, gate_sem = refs
        step = step_ref[span_id]
        first = pl.multiple_of(step - step % GATE_ROWS, GATE_ROWS)
        fetch = pltpu.make_async_copy(table_ref.at[pl.ds(first, GATE_ROWS)], gate_ref, gate_sem)
        fetch.start()
    elif closes:
        top_in, part_in, gate_ref, out_ref, staged_ref, out_sem = refs
        position = lax.axis_index("seq") * tokens + lax.broadcasted_iota(jnp.int32, (tokens, 1), 0)
        live = (position < valid_ref[span_id]).astype(jnp.float32)
    else:
        top_in, part_in, top_out, part_out = refs

    def run(groups):
        def joined(group, c):
            return jnp.concatenate([kv_refs[i][start:stop, c] for i, start, stop in group], axis=0)

        biases = []
        for group in groups:
            order = [d for i, start, stop in group for d in orders[i][start // tokens : stop // tokens]]
            biases.append(key_bias(order, tokens, n_seq, clip_ref, valid_ref))
        scores, tops, writes = {}, {}, []
        for h in heads:
            query = jnp.concatenate([q_ref[:, c] for c in columns[h * RATIO : (h + 1) * RATIO]], axis=0)
            for g, group in enumerate(groups):
                products = lax.dot_general(
                    query,
                    joined(group, columns[h]),
                    (((1,), (1,)), ((), ())),
                    preferred_element_type=jnp.float32,
                )
                scores[h, g] = products * scale + biases[g]
        for h in heads:
            found = [jnp.max(scores[h, g], axis=1, keepdims=True) for g in range(len(groups))]
            top = jnp.broadcast_to(functools.reduce(jnp.maximum, found), (rows, HEAD_WIDTH))
            tops[h] = top if opens else jnp.maximum(top, top_in[h * rows : (h + 1) * rows, :])
        for h in heads:
            span = slice(h * rows, (h + 1) * rows)
            sums = 0.0
            for g, group in enumerate(groups):
                size = scores[h, g].shape[1]
                shift = jnp.concatenate([tops[h]] * pl.cdiv(size, HEAD_WIDTH), axis=1)[:, :size]
                weights = jnp.exp2(scores[h, g] - shift)
                value = joined(group, columns[KEY_VALUE_HEADS + h])
                value = jnp.concatenate([value, jnp.ones_like(value)], axis=1)
                sums = sums + jnp.dot(
                    weights.astype(jnp.bfloat16), value, preferred_element_type=jnp.float32
                )
            numerator, total = sums[:, :HEAD_WIDTH], sums[:, HEAD_WIDTH:]
            if not opens:
                factor = jnp.exp2(top_in[span, :] - tops[h])
                total = total + factor
                numerator = numerator + part_in[span, :] * factor
            result = numerator * (1.0 / total)
            if not closes:
                top_out[span, :] = tops[h] + jnp.log2(total)
                part_out[span, :] = result
                continue
            for r in range(RATIO):
                c = columns[h * RATIO + r]
                part = result[r * tokens : (r + 1) * tokens]
                staged_ref[:, c] = (part * gate_ref[:, c] * live).astype(out_ref.dtype)
            if h % 2 == 0:
                continue
            group = slice((h - 1) * RATIO * HEAD_WIDTH, (h + 1) * RATIO * HEAD_WIDTH)
            writes.append(
                pltpu.make_async_copy(staged_ref.at[:, group], out_ref.at[:, group], out_sem.at[h])
            )
            writes[-1].start()
        for write in writes:
            write.wait()

    run(groups)
    if opens:
        fetch.wait()
        chosen = lax.broadcasted_iota(jnp.int32, (GATE_ROWS, 1), 0) == step % GATE_ROWS
        gate_out[...] = jnp.sum(jnp.where(chosen, gate_ref[...], 0.0), axis=0, keepdims=True)


def attend(scalars, queries, keyvals, orders, groups, n_seq, stage, *carried):
    rows = QUERY_HEADS * queries.shape[0]
    keys = sum(kv.shape[0] for kv in keyvals)
    smem, vmem = pl.BlockSpec(memory_space=pltpu.SMEM), pl.BlockSpec(memory_space=pltpu.VMEM)
    anywhere = pl.BlockSpec(memory_space=pl.ANY)
    operands = [queries, *keyvals, *carried]
    in_specs = [smem] * len(scalars) + [vmem] * len(operands)
    scratch = []
    if stage == "last":
        out_shape, out_specs = jax.ShapeDtypeStruct(queries.shape, jnp.bfloat16), anywhere
        scratch = [
            pltpu.VMEM(queries.shape, jnp.bfloat16),
            pltpu.SemaphoreType.DMA((KEY_VALUE_HEADS,)),
        ]
    else:
        out_shape = [jax.ShapeDtypeStruct((rows, HEAD_WIDTH), jnp.float32)] * 2
        out_specs = [vmem, vmem]
    if stage == "first":
        in_specs[-1] = anywhere
        out_shape.append(jax.ShapeDtypeStruct((1, queries.shape[1]), jnp.float32))
        out_specs.append(vmem)
        scratch = [pltpu.VMEM((GATE_ROWS, queries.shape[1]), jnp.float32), pltpu.SemaphoreType.DMA]
    return pl.pallas_call(
        functools.partial(attend_kernel, orders, groups, stage, n_seq),
        out_shape=out_shape,
        in_specs=in_specs,
        out_specs=out_specs,
        scratch_shapes=scratch,
        compiler_params=pltpu.CompilerParams(vmem_limit_bytes=40 * 1024 * 1024),
        cost_estimate=pl.CostEstimate(
            flops=4 * rows * keys * HEAD_WIDTH,
            bytes_accessed=keys * 2 * KEY_WIDTH * 2,
            transcendentals=rows * keys,
        ),
    )(*scalars, *operands)


def streamed_kernel(place_ref, q_ref, kv_ref, bias_ref, gate_ref, out_ref, top_ref, total_ref, numerator_ref):
    tokens = q_ref.shape[0]
    rows = RATIO * tokens
    scale = LOG2E / math.sqrt(HEAD_WIDTH)

    @pl.when(pl.program_id(0) == 0)
    def _():
        top_ref[...] = jnp.full_like(top_ref, NEGATIVE)
        total_ref[...] = jnp.zeros_like(total_ref)
        numerator_ref[...] = jnp.zeros_like(numerator_ref)

    for head in range(KEY_VALUE_HEADS):
        first = head * RATIO
        span = slice(head * rows, (head + 1) * rows)
        columns = [slice((first + r) * HEAD_WIDTH, (first + r + 1) * HEAD_WIDTH) for r in range(RATIO)]
        query = jnp.concatenate([q_ref[:, c] for c in columns], axis=0)
        key = kv_ref[:, head * HEAD_WIDTH : (head + 1) * HEAD_WIDTH]
        value = kv_ref[:, KEY_WIDTH + head * HEAD_WIDTH : KEY_WIDTH + (head + 1) * HEAD_WIDTH]
        scores = lax.dot_general(
            query, key, (((1,), (1,)), ((), ())), preferred_element_type=jnp.float32
        )
        scores = scores * scale + bias_ref[...]
        top = jnp.maximum(top_ref[span, :], jnp.max(scores, axis=1, keepdims=True))
        weights = jnp.exp2(scores - top)
        factor = jnp.exp2(top_ref[span, :] - top)
        top_ref[span, :] = top
        total_ref[span, :] = total_ref[span, :] * factor + jnp.sum(weights, axis=1, keepdims=True)
        numerator_ref[span, :] = numerator_ref[span, :] * factor + jnp.dot(
            weights.astype(jnp.bfloat16), value, preferred_element_type=jnp.float32
        )

    @pl.when(pl.program_id(0) == pl.num_programs(0) - 1)
    def _():
        positions = place_ref[0] + lax.broadcasted_iota(jnp.int32, (tokens, 1), 0)
        live = (positions < place_ref[1]).astype(jnp.float32)
        for h in range(QUERY_HEADS):
            span = slice(h * tokens, (h + 1) * tokens)
            columns = slice(h * HEAD_WIDTH, (h + 1) * HEAD_WIDTH)
            part = numerator_ref[span, :] / total_ref[span, :]
            out_ref[:, columns] = (part * gate_ref[:, columns] * live).astype(out_ref.dtype)


def streamed(place, queries, keyvals, bias, gate):
    rows = QUERY_HEADS * queries.shape[0]
    keys = keyvals.shape[0]
    tile = TILE if keys % TILE == 0 else keys
    whole = pl.BlockSpec(memory_space=pltpu.VMEM)
    return pl.pallas_call(
        streamed_kernel,
        grid=(keys // tile,),
        out_shape=jax.ShapeDtypeStruct(queries.shape, jnp.bfloat16),
        in_specs=[
            pl.BlockSpec(memory_space=pltpu.SMEM),
            whole,
            pl.BlockSpec((tile, keyvals.shape[1]), lambda t: (t, 0)),
            pl.BlockSpec((1, tile), lambda t: (0, t)),
            whole,
        ],
        out_specs=whole,
        scratch_shapes=[
            pltpu.VMEM((rows, 1), jnp.float32),
            pltpu.VMEM((rows, 1), jnp.float32),
            pltpu.VMEM((rows, HEAD_WIDTH), jnp.float32),
        ],
        compiler_params=pltpu.CompilerParams(vmem_limit_bytes=40 * 1024 * 1024),
    )(place, queries, keyvals, bias, gate)


def gathered_whole(n_span, n_seq, queries, keyvals, clip_index, noise_step, valid_count, gate_table):
    tokens = queries.shape[0]
    span_id, seq_id = lax.axis_index("span"), lax.axis_index("seq")
    groups = jnp.arange(n_span, dtype=jnp.int32)
    own = lambda values: jnp.sum(jnp.where(groups == span_id, values, 0))
    limits = jnp.where(clip_index <= own(clip_index), valid_count, 0)
    usable = jnp.arange(n_seq * tokens, dtype=jnp.int32)[None, :] < limits[:, None]
    bias = jnp.where(usable, 0.0, NEGATIVE).astype(jnp.float32).reshape(1, -1)
    gate = lax.dynamic_slice(gate_table, (own(noise_step), 0), (1, gate_table.shape[1]))
    place = jnp.stack([seq_id * tokens, own(valid_count)])
    rows = lax.all_gather(lax.all_gather(keyvals, "seq", tiled=True), "span", tiled=True)
    return streamed(place, queries, rows, bias, gate)


def per_device(n_span, n_seq, queries, keyvals, clip_index, noise_step, valid_count, gate_table):
    devices = n_span * n_seq
    tokens = queries.shape[0]
    far = [4 * i for i in range(n_seq // 4)]
    if n_span != 2 or len(far) != 4:
        return gathered_whole(
            n_span, n_seq, queries, keyvals, clip_index, noise_step, valid_count, gate_table
        )

    def exchange(block, distance):
        pairs = [(i, i ^ distance) for i in range(devices)]
        return lax.ppermute(block, ("span", "seq"), pairs)

    plane = [n_seq + 2, 2, n_seq]
    away = jnp.concatenate([exchange(keyvals, d) for d in far[2:]], axis=0)
    column = exchange(keyvals, far[1])
    home = jnp.concatenate([keyvals] + [exchange(keyvals, d) for d in plane], axis=0)
    near = jnp.concatenate([column, exchange(home[tokens:], far[1])], axis=0)
    away = jnp.concatenate([away] + [exchange(away, d) for d in plane], axis=0)
    home_order = [0] + plane
    near_order = [far[1] ^ p for p in home_order]
    away_order = [p ^ z for p in home_order for z in far[2:]]
    twin = lambda order: [d ^ 1 for d in order]
    scalars = (clip_index, valid_count, noise_step)
    whole = lambda *parts: [(i, 0, part.shape[0]) for i, part in enumerate(parts)]
    *state, gate = attend(
        scalars, queries, [home], [home_order], [whole(home)], n_seq, "first", gate_table
    )
    near, _ = lax.optimization_barrier((near, state[0]))
    both = exchange(jnp.concatenate([home, near], axis=0), 1)
    twins = [exchange(away, 1), both]
    orders, groups = [away_order, near_order], [whole(away), [(1, 0, near.shape[0])]]
    state = attend(scalars, queries, [away, near], orders, groups, n_seq, "middle", *state)
    orders = [twin(away_order), twin(home_order + near_order)]
    groups = [whole(away), [(1, 0, both.shape[0])]]
    return attend(scalars, queries, twins, orders, groups, n_seq, "last", *state, gate)


def solution(mesh):
    return jax.shard_map(
        functools.partial(per_device, mesh.shape["span"], mesh.shape["seq"]),
        mesh=mesh,
        in_specs=(P(("span", "seq"), None), P(("span", "seq"), None), P(), P(), P(), P()),
        out_specs=P(("span", "seq"), None),
        check_vma=False,
    )
```
